128 devices in a mesh: lat: 16 (over x, y_hi, core), lon: 8 (over y_lo, z).
Axes of the slice: x: 4, y: 4 (y_hi: 2, y_lo: 2; y = y_hi * 2 + y_lo), z: 4, core: 2. Of those that a mesh axis runs over, the one named last changes fastest.
Arguments:
- tokens: bfloat16 [256, 256, 1024], P('lat', 'lon'), may hold values from -6 to 6
- pad_rows: int32 [256], replicated, may hold values from 0 to 1, as said below
- land_sea: int32 [32, 32, 4], P('lat', 'lon'), may hold values from 0 to 1
- win_gain: float32 [1024], replicated, may hold values from 0.5 to 1.5
- win_query: bfloat16 [1024, 1024], replicated, as said below
- win_key: bfloat16 [1024, 1024], replicated, as said below
- win_value: bfloat16 [1024, 1024], replicated, may hold values from -0.1875 to 0.1875
- win_out: bfloat16 [1024, 1024], replicated, may hold values from -0.1875 to 0.1875
- grid_gain: float32 [1024], replicated, may hold values from 0.5 to 1.5
- grid_query: bfloat16 [1024, 1024], replicated, as said below
- grid_key: bfloat16 [1024, 1024], replicated, as said below
- grid_value: bfloat16 [1024, 1024], replicated, may hold values from -0.1875 to 0.1875
- grid_out: bfloat16 [1024, 1024], replicated, may hold values from -0.1875 to 0.1875
Outputs:
- mixed: bfloat16 [256, 256, 1024], P('lat', 'lon')
The draws below stay inside these ranges and needn't reach their ends.
Inputs may be any that keep to these rules, and one draw needn't show every extreme that they name: pad_rows is 0 on the first 0 to 7 rows and on the final 1 to 7 rows of the grid, and 1 on all others. `win_query`: a projection matrix. `win_key`: a projection matrix. `grid_query`: a projection matrix. `grid_key`: a projection matrix.
All inputs are finite; a program needn't handle non-finite values.
Results may differ from the reference program's by a relative error of at most 0.013.
Values may be sent and summed in bfloat16 or wider, within the bound.
No kernel may reach another device: no remote copies, remote signals or barrier semaphores. Data moves between devices by JAX's collectives and lax.ppermute only.
A program may use at most 128 MiB of HBM per device.

```python
import math
import jax
import jax.numpy as jnp
from jax import lax

D = 1024
HEADS = 16
GROUPS = 4
WIN = 8
SHIFT = 4
HL = 16
WL = 32
H = 256
W = 256
N_LAT = 16
N_LON = 8


def qk_pair(key, low_scale, high_scale):
    first = jax.random.normal(jax.random.fold_in(key, 1), (D, D), jnp.float32)
    second = jax.random.normal(jax.random.fold_in(key, 2), (D, D), jnp.float32)
    columns = jnp.exp(jax.random.uniform(jax.random.fold_in(key, 3), (D,), jnp.float32, math.log(low_scale), math.log(high_scale)))
    base_scale = columns * D ** (-0.5)
    query_mat = first * base_scale
    key_mat = second * base_scale
    return (query_mat.astype(jnp.bfloat16), key_mat.astype(jnp.bfloat16))


def draw_win_query(key, part):
    return qk_pair(jax.random.fold_in(key, 101), 1.0, 1.0)[0]


def draw_win_key(key, part):
    return qk_pair(jax.random.fold_in(key, 101), 1.0, 1.0)[1]


def draw_grid_query(key, part):
    return qk_pair(jax.random.fold_in(key, 202), 1.0, 1.0)[0]


def draw_grid_key(key, part):
    return qk_pair(jax.random.fold_in(key, 202), 1.0, 1.0)[1]


def draw_pad_rows(key, part):
    key = jax.random.fold_in(key, 7)
    top_count = jax.random.randint(jax.random.fold_in(key, 1), (), 0, WIN)
    bottom_count = jax.random.randint(jax.random.fold_in(key, 2), (), 1, WIN)
    row_index = jnp.arange(H, dtype=jnp.int32)
    inside = (row_index >= top_count) & (row_index < H - bottom_count)
    return inside.astype(jnp.int32)


def draw_land_sea(key, part):
    key = jax.random.fold_in(key, 9)
    tile_total = H // WIN
    tile_index = jnp.arange(tile_total, dtype=jnp.int32)
    thresholds = 3 + 12 * tile_index // tile_total
    random_ints = jax.random.randint(key, (tile_total, W // WIN, GROUPS), 0, 16)
    return (random_ints < thresholds[:, None, None]).astype(jnp.int32)


def steps_of(stream_key, dims, split, low, top_value):
    gain, own = 1.0, jax.random.fold_in(stream_key, 6)
    for axis_at, blocks in split:
        heights = jnp.exp(jax.random.uniform(jax.random.fold_in(own, axis_at), (blocks,), jnp.float32, low / len(split), top_value / len(split)))
        gain = gain * jnp.repeat(heights, dims[axis_at] // blocks).reshape([-1 if axis == axis_at else 1 for axis in range(len(dims))])
    return gain


def noise(rng, dims, scale, bound, pieces=(), held_as=jnp.bfloat16):
    level = steps_of(rng, dims, pieces, -0.22, 0.18) if pieces else 1.0
    drawn = jax.random.normal(rng, dims, jnp.float32) * scale * level
    return jnp.minimum(jnp.maximum(drawn, -bound), bound).astype(held_as)


def setup_inputs(seed: int = 0) -> dict:
    key_of = jax.random.split(jax.random.key(seed), 14)
    tokens = noise(key_of[0], (H, W, D), 1.0, 6.0, ((0, 16), (1, 8)))
    pad_rows = draw_pad_rows(jax.random.fold_in(key_of[13], 71), 0)
    land_sea = draw_land_sea(jax.random.fold_in(key_of[13], 71), 0)
    win_gain = jnp.clip(1.0 + 0.1 * jax.random.normal(key_of[3], (D,), jnp.float32), 0.5, 1.5)
    win_query = draw_win_query(jax.random.fold_in(key_of[13], 71), 0)
    win_key = draw_win_key(jax.random.fold_in(key_of[13], 71), 0)
    win_value = noise(key_of[6], (D, D), D ** -0.5, 0.1875)
    win_out = noise(key_of[7], (D, D), D ** -0.5, 0.1875)
    grid_gain = jnp.clip(1.0 + 0.1 * jax.random.normal(key_of[8], (D,), jnp.float32), 0.5, 1.5)
    grid_query = draw_grid_query(jax.random.fold_in(key_of[13], 71), 0)
    grid_key = draw_grid_key(jax.random.fold_in(key_of[13], 71), 0)
    grid_value = noise(key_of[11], (D, D), D ** -0.5, 0.1875)
    grid_out = noise(key_of[12], (D, D), D ** -0.5, 0.1875)
    return dict(tokens=tokens, pad_rows=pad_rows, land_sea=land_sea, win_gain=win_gain, win_query=win_query, win_key=win_key, win_value=win_value, win_out=win_out, grid_gain=grid_gain, grid_query=grid_query, grid_key=grid_key, grid_value=grid_value, grid_out=grid_out)


epsilon = 1e-06

def rms_scale(inputs, gain_row):
    floats = inputs.astype(jnp.float32)
    mean_sq = lax.optimization_barrier(jnp.mean(floats * floats, axis=-1, keepdims=True))
    return (floats * lax.rsqrt(mean_sq + epsilon) * gain_row).astype(jnp.bfloat16)

def project(inputs, matrix):
    return jnp.dot(inputs, matrix, preferred_element_type=jnp.float32).astype(jnp.bfloat16)

def attend(query_rows, key_rows, value_rows, usable):
    group_count, query_count, features = query_rows.shape
    key_count = key_rows.shape[1]
    head_size = features // HEADS
    query_heads = query_rows.astype(jnp.float32).reshape(group_count, query_count, HEADS, head_size)
    key_heads = key_rows.astype(jnp.float32).reshape(group_count, key_count, HEADS, head_size)
    value_heads = value_rows.astype(jnp.float32).reshape(group_count, key_count, HEADS, head_size)
    scores = jnp.einsum('blhd,bshd->bhls', query_heads, key_heads) * (1.0 / math.sqrt(head_size))
    scores = jnp.where(usable[:, None, None, :], scores, -jnp.inf)
    largest = lax.optimization_barrier(jnp.max(scores, axis=-1, keepdims=True))
    exponentials = jnp.exp(scores - largest)
    attention = (exponentials / lax.optimization_barrier(jnp.sum(exponentials, axis=-1, keepdims=True))).astype(jnp.bfloat16)
    return jnp.einsum('bhls,bshd->blhd', attention.astype(jnp.float32), value_heads)

def window_mix(normed, pad_band, land_band, query_mat, key_mat, value_mat, out_mat):
    height, breadth, features = normed.shape
    tile_rows = height // WIN
    tile_cols = breadth // WIN
    tile_set = normed.reshape(tile_rows, WIN, tile_cols, WIN, features).transpose(0, 2, 1, 3, 4)
    tile_set = tile_set.reshape(tile_rows * tile_cols, WIN * WIN, features)
    usable = jnp.repeat(pad_band.reshape(tile_rows, WIN) > 0, WIN, axis=1)
    usable = jnp.broadcast_to(usable[:, None, :], (tile_rows, tile_cols, WIN * WIN)).reshape(tile_rows * tile_cols, WIN * WIN)
    heads_out = attend(project(tile_set, query_mat), project(tile_set, key_mat), project(tile_set, value_mat), usable)
    head_gate = jnp.repeat(land_band.reshape(tile_rows * tile_cols, GROUPS), HEADS // GROUPS, axis=1).astype(jnp.float32)
    heads_out = (heads_out * head_gate[:, None, :, None]).astype(jnp.bfloat16)
    heads_out = heads_out.reshape(tile_rows * tile_cols, WIN * WIN, features)
    update = jnp.dot(heads_out, out_mat, preferred_element_type=jnp.float32)
    update = update.reshape(tile_rows, tile_cols, WIN, WIN, features).transpose(0, 2, 1, 3, 4)
    return update.reshape(height, breadth, features)

def reference(tokens, pad_rows, land_sea, win_gain, win_query, win_key, win_value, win_out, grid_gain, grid_query, grid_key, grid_value, grid_out):
    normed = rms_scale(tokens, win_gain)
    rolled = jnp.roll(normed, -SHIFT, axis=1)
    band_stack = rolled.reshape(H // WIN, WIN, W, D)
    pad_bands = pad_rows.reshape(H // WIN, WIN)

    def one_band(entries):
        band_rows, pad_band, land_band = entries
        return window_mix(band_rows, pad_band, land_band, win_query, win_key, win_value, win_out)
    update = lax.map(one_band, (band_stack, pad_bands, land_sea)).reshape(H, W, D)
    after_window = (tokens.astype(jnp.float32) + jnp.roll(update, SHIFT, axis=1)).astype(jnp.bfloat16)
    grid_normed = rms_scale(after_window, grid_gain)
    members = N_LAT * N_LON
    grouped = grid_normed.reshape(N_LAT, HL, N_LON, WL, D).transpose(1, 3, 0, 2, 4).reshape(HL, WL, members, D)
    pad_grid = pad_rows.reshape(N_LAT, HL).T

    def one_row(entries):
        group_row, pad_row = entries
        usable = jnp.broadcast_to(jnp.repeat(pad_row > 0, N_LON)[None, :], (WL, members))
        heads_out = attend(project(group_row, grid_query), project(group_row, grid_key), project(group_row, grid_value), usable)
        heads_out = heads_out.astype(jnp.bfloat16).reshape(WL, members, D)
        return jnp.dot(heads_out, grid_out, preferred_element_type=jnp.float32)
    grid_update = lax.map(one_row, (grouped, pad_grid))
    grid_update = grid_update.reshape(HL, WL, N_LAT, N_LON, D).transpose(2, 0, 3, 1, 4).reshape(H, W, D)
    return (after_window.astype(jnp.float32) + grid_update).astype(jnp.bfloat16)
```

```python
import functools
import math

import jax
import jax.numpy as jnp
from jax import lax
from jax.experimental import pallas as pl
from jax.experimental.pallas import tpu as pltpu
from jax.sharding import PartitionSpec as P

HEADS = 16
GROUPS = 4
WIN = 8
SHIFT = 4
EPSILON = 1e-06
MASKED = -1e30
BF16 = jnp.bfloat16
F32 = jnp.float32
I32 = jnp.int32


def iota(shape, axis):
    return lax.broadcasted_iota(I32, shape, axis)


def one_hot(hits):
    return jnp.where(hits, 1.0, 0.0).astype(BF16)


def matmul(left, right):
    return jnp.dot(left, right, preferred_element_type=F32)


def matmul_nt(left, right):
    return lax.dot_general(left, right, (((1,), (1,)), ((), ())), preferred_element_type=F32)


def norm(rows, gain):
    mean_sq = jnp.mean(rows * rows, axis=-1, keepdims=True)
    return (rows * lax.rsqrt(mean_sq + EPSILON) * gain).astype(BF16)


def usable_bias(pad_ref, wanted_row):
    lanes = wanted_row.shape[1]
    pads = jnp.broadcast_to(pad_ref[...].astype(F32).astype(BF16), (16, pad_ref.shape[1]))
    picks = one_hot(iota((pad_ref.shape[1], lanes), 0) == wanted_row)
    return jnp.where(matmul(pads, picks)[:1] > 0.5, 0.0, MASKED)


def tile_place(part, row):
    if part == 0:
        tile = row // 64
        return (tile // 2) * 8 + (row // 8) % 8, (tile % 2) * 8 + row % 8
    half = row - 128
    whole_row, whole_col = (row // 64) * 8 + (row // 8) % 8, row % 8
    half_row, half_col = (half % 64) // 4, 8 + (half // 64) * 4 + half % 4
    whole = row < 128
    return jnp.where(whole, whole_row, half_row), jnp.where(whole, whole_col, half_col)


def window_kernel(part, *refs):
    if part == 0:
        tok_ref, pad_ref, land_ref, gain_ref, *refs = refs
    else:
        tok_ref, right_ref, left_ref, pad_ref, land_ref, land_left_ref, gain_ref, *refs = refs
    wq_hbm, wk_hbm, wv_hbm, wo_hbm, out_ref, weights, q_ref, k_ref, v_ref, heads_ref, sems = refs
    copies = [
        pltpu.make_async_copy(source, weights.at[n], sems.at[n])
        for n, source in enumerate((wq_hbm, wk_hbm, wv_hbm, wo_hbm))
    ]
    for copy in copies:
        copy.start()
    cells, width = tok_ref.shape
    rows = cells // 2
    row, col = tile_place(part, iota((rows, 1), 0))
    source = row * 32 + (4 + 16 * part + col) % 32
    order = one_hot(iota((rows, cells), 1) == source)
    x = matmul(order, tok_ref[...])
    gain = gain_ref[...]
    normed = norm(x, gain)
    if part == 1:
        halo = jnp.concatenate([right_ref[...], left_ref[...]], axis=0).astype(F32)
        all_normed = jnp.concatenate([normed, norm(halo, gain)], axis=0)
    else:
        all_normed = normed
    head_size = width // HEADS
    copies[0].wait()
    factor = math.log2(math.e) / math.sqrt(head_size)
    q_ref[...] = (matmul(normed, weights[0]) * factor).astype(BF16)
    copies[1].wait()
    k_ref[...] = matmul(all_normed, weights[1]).astype(BF16)
    copies[2].wait()
    v_ref[...] = matmul(all_normed, weights[2]).astype(BF16)

    quad = 4 * head_size
    first = lax.axis_index("lat") * 16
    key_lane = iota((1, quad), 1) % 64
    biases = {}
    for tile_row in range(2):
        biases[tile_row, True] = usable_bias(pad_ref, first + tile_row * 8 + key_lane // 8)
        if part == 1:
            biases[tile_row, False] = usable_bias(
                pad_ref, first + tile_row * 8 + (key_lane % 32) // 4
            )
    head_lane = iota((1, quad), 1) // head_size
    masks = [one_hot(head_lane == h) for h in range(4)]
    ones = one_hot(iota((quad, quad), 0) // 64 == iota((quad, quad), 1) // head_size)
    lower = iota((1, 128), 1) < 64

    def spread(block):
        return jnp.concatenate([block * mask for mask in masks], axis=0)

    tiles = []
    if part == 0:
        for tile_row in range(2):
            for tile_col in range(2):
                start = (tile_row * 2 + tile_col) * 64
                tiles.append((start, 64, ((start, 64),), tile_row, True, (land_ref, tile_col)))
    else:
        for tile_row in range(2):
            start = tile_row * 64
            tiles.append((start, 64, ((start, 64),), tile_row, True, (land_ref, 2)))
        for side in range(2):
            for tile_row in range(2):
                start = 128 + (side * 2 + tile_row) * 32
                spans = ((start, 32), (start + 128, 32))
                gates = (land_ref, 3) if side == 0 else (land_left_ref, 0)
                tiles.append((start, 32, spans, tile_row, False, gates))
    for start, count, spans, tile_row, whole, (gate_ref, tile_col) in tiles:
        for group in range(GROUPS):
            lanes = slice(group * quad, (group + 1) * quad)
            query = q_ref[start : start + count, lanes]
            key = jnp.concatenate([k_ref[s : s + n, lanes] for s, n in spans], axis=0)
            value = jnp.concatenate([v_ref[s : s + n, lanes] for s, n in spans], axis=0)
            scores = matmul_nt(query, spread(key)) + biases[tile_row, whole]
            exps = []
            for block in range(2):
                part_scores = scores[:, block * 128 : (block + 1) * 128]
                low = jnp.max(jnp.where(lower, part_scores, -jnp.inf), axis=1, keepdims=True)
                high = jnp.max(jnp.where(lower, -jnp.inf, part_scores), axis=1, keepdims=True)
                exps.append(jnp.exp2(part_scores - jnp.where(lower, low, high)).astype(BF16))
            weight = jnp.concatenate(exps, axis=1)
            total = matmul(weight, ones)
            gate = gate_ref[tile_row, tile_col, group].astype(F32)
            heads = matmul(weight, spread(value)) / total * gate
            heads_ref[start : start + count, lanes] = heads.astype(BF16)
    copies[3].wait()
    after = (x + matmul(heads_ref[...], weights[3])).astype(BF16)
    row, col = tile_place(part, iota((1, rows), 1))
    back = one_hot(iota((rows, rows), 0) == row * 16 + col)
    out_ref[...] = matmul(back, after).astype(BF16)


def window_part(part, tokens, halos, pads, land_sea, land_left, gain, weights):
    cells, width = tokens.shape
    rows = cells // 2
    key_rows = rows if part == 0 else rows + 128
    vmem = pl.BlockSpec(memory_space=pltpu.VMEM)
    smem = pl.BlockSpec(memory_space=pltpu.SMEM)
    hbm = pl.BlockSpec(memory_space=pl.ANY)
    if part == 0:
        args, specs = (tokens, pads, land_sea, gain), [vmem, vmem, smem, vmem]
    else:
        args = (tokens, *halos, pads, land_sea, land_left, gain)
        specs = [vmem, vmem, vmem, vmem, smem, smem, vmem]
    return pl.pallas_call(
        functools.partial(window_kernel, part),
        out_shape=jax.ShapeDtypeStruct((rows, width), BF16),
        in_specs=specs + [hbm] * 4,
        out_specs=vmem,
        scratch_shapes=[
            pltpu.VMEM((4, width, width), BF16),
            pltpu.VMEM((rows, width), BF16),
            pltpu.VMEM((key_rows, width), BF16),
            pltpu.VMEM((key_rows, width), BF16),
            pltpu.VMEM((rows, width), BF16),
            pltpu.SemaphoreType.DMA((4,)),
        ],
        compiler_params=pltpu.CompilerParams(vmem_limit_bytes=40 * 2**20),
        cost_estimate=pl.CostEstimate(
            flops=8 * rows * width * width, bytes_accessed=12 * 2**20, transcendentals=rows * 1024
        ),
        name=f"window_part{part}",
    )(*args, *weights)


def grid_kernel(cell_ref, pad_ref, gain_ref, *refs):
    wq_hbm, wk_hbm, wv_hbm, wo_hbm, out_ref, weights, q_ref, k_ref, v_ref, heads_ref, sems = refs
    copies = [
        pltpu.make_async_copy(source, weights.at[n], sems.at[n])
        for n, source in enumerate((wq_hbm, wk_hbm, wv_hbm, wo_hbm))
    ]
    for copy in copies:
        copy.start()
    rows, width = cell_ref.shape
    members = 128
    groups = rows // members
    row = iota((rows, 1), 0)
    order = one_hot(iota((rows, rows), 1) == (row % members) * groups + row // members)
    x = matmul(order, cell_ref[...])
    normed = norm(x, gain_ref[...])
    head_size = width // HEADS
    copies[0].wait()
    factor = math.log2(math.e) / math.sqrt(head_size)
    q_ref[...] = (matmul(normed, weights[0]) * factor).astype(BF16)
    copies[1].wait()
    k_ref[...] = matmul(normed, weights[1]).astype(BF16)
    copies[2].wait()
    v_ref[...] = matmul(normed, weights[2]).astype(BF16)

    pair = 2 * head_size
    key_lane = iota((1, 2 * members), 1) % members
    bias = usable_bias(pad_ref, (key_lane // 8) * 16 + lax.axis_index("lat"))
    masks = [one_hot(iota((1, pair), 1) // head_size == h) for h in range(2)]
    ones = one_hot(
        iota((2 * members, pair), 0) // members == iota((2 * members, pair), 1) // head_size
    )

    def spread(block):
        return jnp.concatenate([block * mask for mask in masks], axis=0)

    for group in range(groups):
        span = slice(group * members, (group + 1) * members)
        for two in range(HEADS // 2):
            lanes = slice(two * pair, (two + 1) * pair)
            scores = matmul_nt(q_ref[span, lanes], spread(k_ref[span, lanes])) + bias
            exps = []
            for half in range(2):
                head_scores = scores[:, half * members : (half + 1) * members]
                largest = jnp.max(head_scores, axis=1, keepdims=True)
                exps.append(jnp.exp2(head_scores - largest).astype(BF16))
            weight = jnp.concatenate(exps, axis=1)
            both = jnp.concatenate([spread(v_ref[span, lanes]), ones], axis=1)
            sums = matmul(weight, both)
            heads_ref[span, lanes] = (sums[:, :pair] / sums[:, pair:]).astype(BF16)
    copies[3].wait()
    mixed = (x + matmul(heads_ref[...], weights[3])).astype(BF16)
    col = iota((1, rows), 1)
    back = one_hot(iota((rows, rows), 0) == (col % members) * groups + col // members)
    out_ref[...] = matmul(back, mixed).astype(BF16)


def grid_part(cells, pads, gain, weights):
    rows, width = cells.shape
    vmem = pl.BlockSpec(memory_space=pltpu.VMEM)
    hbm = pl.BlockSpec(memory_space=pl.ANY)
    return pl.pallas_call(
        grid_kernel,
        out_shape=jax.ShapeDtypeStruct((rows, width), BF16),
        in_specs=[vmem] * 3 + [hbm] * 4,
        out_specs=vmem,
        scratch_shapes=[
            pltpu.VMEM((4, width, width), BF16),
            pltpu.VMEM((rows, width), BF16),
            pltpu.VMEM((rows, width), BF16),
            pltpu.VMEM((rows, width), BF16),
            pltpu.VMEM((rows, width), BF16),
            pltpu.SemaphoreType.DMA((4,)),
        ],
        compiler_params=pltpu.CompilerParams(vmem_limit_bytes=40 * 2**20),
        cost_estimate=pl.CostEstimate(
            flops=8 * rows * width * width, bytes_accessed=10 * 2**20, transcendentals=rows * 2048
        ),
        name="grid_part",
    )(cells, pads, gain, *weights)


def from_behind(block, axis, distance):
    devices = range(lax.axis_size(axis))
    route = [((i - distance) % len(devices), i) for i in devices]
    return lax.ppermute(block, axis, route)


def exchange(rows):
    count, width = rows.shape
    members = lax.axis_size("lat") * lax.axis_size("lon")
    blocks = rows.reshape(members, count // members, width)
    moved = lax.all_to_all(blocks, ("lat", "lon"), split_axis=0, concat_axis=0, tiled=True)
    return moved.reshape(count, width)


def local(
    tokens,
    pad_rows,
    land_sea,
    win_gain,
    win_query,
    win_key,
    win_value,
    win_out,
    grid_gain,
    grid_query,
    grid_key,
    grid_value,
    grid_out,
):
    height, breadth, width = tokens.shape
    flat = tokens.reshape(height * breadth, width)
    pads = pad_rows.reshape(1, -1)
    right = from_behind(tokens[:, :SHIFT], "lon", -1).reshape(height * SHIFT, width)
    left = from_behind(tokens[:, breadth - SHIFT :], "lon", 1).reshape(height * SHIFT, width)
    land_left = from_behind(land_sea[:, -1:], "lon", 1)
    win_weights = (win_query, win_key, win_value, win_out)
    grid_weights = (grid_query, grid_key, grid_value, grid_out)
    results = []
    for part in range(2):
        after = window_part(
            part,
            flat,
            (right, left),
            pads,
            land_sea,
            land_left,
            win_gain.reshape(1, -1),
            win_weights,
        )
        cells = exchange(after)
        mixed = grid_part(cells, pads, grid_gain.reshape(1, -1), grid_weights)
        results.append(exchange(mixed).reshape(height, breadth // 2, width))
    inner, outer = results
    return jnp.concatenate([outer[:, 12:], inner, outer[:, :12]], axis=1)


def solution(mesh):
    whole = P()
    split = P("lat", "lon", None)
    placed = (split, whole, split) + (whole,) * 10
    return jax.shard_map(local, mesh=mesh, in_specs=placed, out_specs=split, check_vma=False)
```

```python
import functools
import math

import jax
import jax.numpy as jnp
from jax import lax
from jax.experimental import pallas as pl
from jax.experimental.pallas import tpu as pltpu
from jax.sharding import PartitionSpec as P

HEADS = 16
GROUPS = 4
WIN = 8
SHIFT = 4
EPSILON = 1e-06
MASKED = -1e30
BF16 = jnp.bfloat16
F32 = jnp.float32
I32 = jnp.int32


def iota(shape, axis):
    return lax.broadcasted_iota(I32, shape, axis)


def one_hot(hits):
    return jnp.where(hits, 1.0, 0.0).astype(BF16)


def matmul(left, right):
    return jnp.dot(left, right, preferred_element_type=F32)


def matmul_nt(left, right):
    return lax.dot_general(left, right, (((1,), (1,)), ((), ())), preferred_element_type=F32)


def norm(rows, gain):
    mean_sq = jnp.mean(rows * rows, axis=-1, keepdims=True)
    return (rows * lax.rsqrt(mean_sq + EPSILON) * gain).astype(BF16)


def usable_bias(pad_ref, wanted_row):
    lanes = wanted_row.shape[1]
    pads = jnp.broadcast_to(pad_ref[...].astype(F32).astype(BF16), (16, pad_ref.shape[1]))
    picks = one_hot(iota((pad_ref.shape[1], lanes), 0) == wanted_row)
    return jnp.where(matmul(pads, picks)[:1] > 0.5, 0.0, MASKED)


def fetch(pairs, sems):
    copies = [
        pltpu.make_async_copy(source, target, sems.at[n]) for n, (source, target) in enumerate(pairs)
    ]
    for copy in copies:
        copy.start()
    return copies


def cross(upper, lower):
    first = iota((1, 8, 1), 1) < 4
    return (
        jnp.where(first, upper, jnp.roll(lower, 4, axis=1)),
        jnp.where(first, jnp.roll(upper, 4, axis=1), lower),
    )


def to_blocks(rows):
    count, width = rows.shape
    half = width // 2
    tiles = rows.reshape(count // 8, 8, width)
    even, odd = cross(tiles[:, :, :half], tiles[:, :, half:])
    return jnp.stack([even, odd], axis=1).reshape(2 * count, half)


def from_blocks(blocks):
    count, half = blocks.shape
    tiles = blocks.reshape(count // 16, 2, 8, half)
    first, second = cross(tiles[:, 0], tiles[:, 1])
    return jnp.concatenate([first, second], axis=2).reshape(count // 2, 2 * half)


def project(rows, weight, target_ref, factor=None):
    product = matmul(rows, weight[...])
    if factor is not None:
        product = product * factor
    target_ref[...] = product.astype(BF16)


def query_factor(head_size):
    return math.log2(math.e) / math.sqrt(head_size)


def window_attention(tiles, pad_ref, land_ref, q_ref, k_ref, v_ref, heads_ref):
    width = q_ref.shape[1]
    head_size = width // HEADS
    quad = 4 * head_size
    first = lax.axis_index("lat") * 16
    key_lane = iota((1, quad), 1) % 64
    biases = [usable_bias(pad_ref, first + band * 8 + key_lane // 8) for band in range(2)]
    head_lane = iota((1, quad), 1) // head_size
    masks = [one_hot(head_lane == h) for h in range(4)]
    ones = one_hot(iota((quad, quad), 0) // 64 == iota((quad, quad), 1) // head_size)
    lower = iota((1, 128), 1) < 64

    def spread(block):
        return jnp.concatenate([block * mask for mask in masks], axis=0)

    for tile, (band, tile_col) in enumerate(tiles):
        span = slice(tile * 64, (tile + 1) * 64)
        for group in range(GROUPS):
            lanes = slice(group * quad, (group + 1) * quad)
            scores = matmul_nt(q_ref[span, lanes], spread(k_ref[span, lanes])) + biases[band]
            exps = []
            for block in range(2):
                part_scores = scores[:, block * 128 : (block + 1) * 128]
                low = jnp.max(jnp.where(lower, part_scores, -jnp.inf), axis=1, keepdims=True)
                high = jnp.max(jnp.where(lower, -jnp.inf, part_scores), axis=1, keepdims=True)
                exps.append(jnp.exp2(part_scores - jnp.where(lower, low, high)).astype(BF16))
            weight = jnp.concatenate(exps, axis=1)
            total = matmul(weight, ones)
            gate = land_ref[band, tile_col, group].astype(F32)
            heads = matmul(weight, spread(v_ref[span, lanes])) / total * gate
            heads_ref[span, lanes] = heads.astype(BF16)


def inner_kernel(
    tok_hbm, pad_hbm, land_hbm, gain_hbm, wq_hbm, wk_hbm, wv_hbm, wo_hbm,
    out_ref, wq_ref, wk_ref, wv_ref, wo_ref,
    tok_ref, pad_ref, land_ref, gain_ref, q_ref, k_ref, v_ref, heads_ref, sems,
):
    copies = fetch(
        [
            (tok_hbm, tok_ref), (gain_hbm, gain_ref), (pad_hbm, pad_ref), (land_hbm, land_ref),
            (wq_hbm, wq_ref), (wk_hbm, wk_ref), (wv_hbm, wv_ref), (wo_hbm, wo_ref),
        ],
        sems,
    )
    cells, width = tok_ref.shape
    rows = heads_ref.shape[0]
    row = iota((rows, 1), 0)
    tile, line, col = row // 64, (row // 8) % 8, row % 8
    source = ((tile // 3) * 8 + line) * 32 + SHIFT + (tile % 3) * 8 + col
    order = one_hot(iota((rows, cells), 1) == source)
    for copy in copies[:4]:
        copy.wait()
    x = matmul(order, tok_ref[...])
    normed = norm(x, gain_ref[...])
    copies[4].wait()
    project(normed, wq_ref, q_ref, query_factor(width // HEADS))
    copies[5].wait()
    project(normed, wk_ref, k_ref)
    copies[6].wait()
    project(normed, wv_ref, v_ref)
    tiles = [(band, tile_col) for band in range(2) for tile_col in range(3)]
    window_attention(tiles, pad_ref, land_ref, q_ref, k_ref, v_ref, heads_ref)
    copies[7].wait()
    out_ref[...] = (x + matmul(heads_ref[...], wo_ref[...])).astype(BF16)


def outer_kernel(
    after_ref, halo_ref, wq_ref, wk_ref, wv_ref, wo_ref,
    tok_hbm, pad_hbm, land_hbm, gain_hbm, gq_hbm, gk_hbm, gv_hbm, go_hbm,
    out_ref, gq_ref, gk_ref, gv_ref, go_ref,
    tok_ref, pad_ref, land_ref, gain_ref, q_ref, k_ref, v_ref, heads_ref, sems,
):
    copies = fetch(
        [
            (tok_hbm, tok_ref), (gain_hbm, gain_ref), (pad_hbm, pad_ref), (land_hbm, land_ref),
            (gq_hbm, gq_ref), (gk_hbm, gk_ref), (gv_hbm, gv_ref), (go_hbm, go_ref),
        ],
        sems,
    )
    cells, width = tok_ref.shape
    halo_rows = halo_ref.shape[0]
    rows = heads_ref.shape[0]
    row = iota((rows, 1), 0)
    line, col = row // 8, row % 8
    own = one_hot(iota((rows, cells), 1) == jnp.where(col < 4, line * 32 + 28 + col, -1))
    halo = one_hot(iota((rows, halo_rows), 1) == jnp.where(col < 4, -1, line * SHIFT + col - 4))
    for copy in copies[:4]:
        copy.wait()
    x = matmul(own, tok_ref[...]) + matmul(halo, halo_ref[...])
    normed = norm(x, gain_ref[...])
    project(normed, wq_ref, q_ref, query_factor(width // HEADS))
    project(normed, wk_ref, k_ref)
    project(normed, wv_ref, v_ref)
    tiles = [(band, 3) for band in range(2)]
    window_attention(tiles, pad_ref, land_ref, q_ref, k_ref, v_ref, heads_ref)
    after = (x + matmul(heads_ref[...], wo_ref[...])).astype(BF16)
    inner_rows = after_ref.shape[0]
    row = iota((1, inner_rows), 1)
    tile, line, col = row // 64, (row // 8) % 8, row % 8
    place = ((tile // 3) * 8 + line) * 32 + SHIFT + (tile % 3) * 8 + col
    inner = one_hot(iota((cells, inner_rows), 0) == place)
    row = iota((1, rows), 1)
    outer = one_hot(iota((cells, rows), 0) == (row // 8) * 32 + (28 + row % 8) % 32)
    both = matmul(inner, after_ref[...]) + matmul(outer, after)
    out_ref[...] = to_blocks(both).astype(BF16)
    for copy in copies[4:]:
        copy.wait()


def in_hbm(arrays):
    return [pltpu.with_memory_space_constraint(a, pltpu.HBM) for a in arrays]


VMEM_SPEC = pl.BlockSpec(memory_space=pltpu.VMEM)
HBM_SPEC = pl.BlockSpec(memory_space=pltpu.HBM)


def call(kernel, name, outs, in_vmem, from_hbm, scratch, rows, exps):
    width = 1024
    return pl.pallas_call(
        kernel,
        out_shape=outs,
        in_specs=[VMEM_SPEC] * len(in_vmem) + [HBM_SPEC] * len(from_hbm),
        out_specs=[VMEM_SPEC] * len(outs),
        scratch_shapes=scratch,
        compiler_params=pltpu.CompilerParams(vmem_limit_bytes=28 * 2**20),
        cost_estimate=pl.CostEstimate(
            flops=8 * rows * width * width, bytes_accessed=10 * 2**20, transcendentals=exps
        ),
        name=name,
    )(*in_vmem, *in_hbm(from_hbm))


def window_part(tokens, halo, pads, land_sea, gain, weights, grid_weights):
    cells, width = tokens.shape
    held = [pltpu.VMEM((width, width), BF16)] * 4
    small = [
        pltpu.VMEM((cells, width), BF16),
        pltpu.VMEM(pads.shape, I32),
        pltpu.SMEM(land_sea.shape, I32),
        pltpu.VMEM(gain.shape, F32),
    ]
    inner, outer = cells * 3 // 4, cells // 4
    sems = pltpu.SemaphoreType.DMA((8,))
    after, *window_weights = call(
        inner_kernel,
        "window_inner",
        [pltpu.VMEM((inner, width), BF16)] + held,
        [],
        [tokens, pads, land_sea, gain, *weights],
        small + [pltpu.VMEM((inner, width), BF16)] * 4 + [sems],
        inner,
        inner * 1024,
    )
    return call(
        outer_kernel,
        "window_outer",
        [jax.ShapeDtypeStruct((2 * cells, width // 2), BF16)] + held,
        [after, halo, *window_weights],
        [tokens, pads, land_sea, gain, *grid_weights],
        small + [pltpu.VMEM((outer, width), BF16)] * 4 + [sems],
        outer,
        outer * 1024,
    )


def grid_kernel(
    block_ref, wq_ref, wk_ref, wv_ref, wo_ref, pad_hbm, gain_hbm,
    out_ref, pad_ref, gain_ref, q_ref, k_ref, v_ref, heads_ref, sems,
):
    copies = fetch([(gain_hbm, gain_ref), (pad_hbm, pad_ref)], sems)
    rows, width = q_ref.shape
    members = 128
    groups = rows // members
    head_size = width // HEADS
    pair = 2 * head_size
    cells = from_blocks(block_ref[...].astype(F32)).astype(BF16)
    row = iota((rows, 1), 0)
    order = one_hot(iota((rows, rows), 1) == (row % members) * groups + row // members)
    x = matmul(order, cells)
    for copy in copies:
        copy.wait()
    normed = norm(x, gain_ref[...])
    project(normed, wq_ref, q_ref, query_factor(head_size))
    project(normed, wk_ref, k_ref)
    project(normed, wv_ref, v_ref)
    key_lane = iota((1, 2 * members), 1) % members
    bias = usable_bias(pad_ref, (key_lane // 8) * 16 + lax.axis_index("lat"))
    masks = [one_hot(iota((1, pair), 1) // head_size == h) for h in range(2)]
    ones = one_hot(
        iota((2 * members, pair), 0) // members == iota((2 * members, pair), 1) // head_size
    )

    def spread(block):
        return jnp.concatenate([block * mask for mask in masks], axis=0)

    for group in range(groups):
        span = slice(group * members, (group + 1) * members)
        for two in range(HEADS // 2):
            lanes = slice(two * pair, (two + 1) * pair)
            scores = matmul_nt(q_ref[span, lanes], spread(k_ref[span, lanes])) + bias
            exps = []
            for half in range(2):
                head_scores = scores[:, half * members : (half + 1) * members]
                largest = jnp.max(head_scores, axis=1, keepdims=True)
                exps.append(jnp.exp2(head_scores - largest).astype(BF16))
            weight = jnp.concatenate(exps, axis=1)
            both = jnp.concatenate([spread(v_ref[span, lanes]), ones], axis=1)
            sums = matmul(weight, both)
            heads_ref[span, lanes] = (sums[:, :pair] / sums[:, pair:]).astype(BF16)
    mixed = (x + matmul(heads_ref[...], wo_ref[...])).astype(BF16)
    col = iota((1, rows), 1)
    member, group = col % members, col // members
    wrapped = jnp.where(lax.axis_index("lon") == 0, 1, 0)
    home = (member // 8) * 8 + (member + wrapped) % 8
    back = one_hot(iota((rows, rows), 0) == home * groups + group)
    out_ref[...] = to_blocks(matmul(back, mixed)).astype(BF16)


def grid_part(blocks, pads, gain, weights):
    rows, width = blocks.shape[0] // 2, blocks.shape[1] * 2
    return call(
        grid_kernel,
        "grid_part",
        [jax.ShapeDtypeStruct(blocks.shape, BF16)],
        [blocks, *weights],
        [pads, gain],
        [pltpu.VMEM(pads.shape, I32), pltpu.VMEM(gain.shape, F32)]
        + [pltpu.VMEM((rows, width), BF16)] * 4
        + [pltpu.SemaphoreType.DMA((2,))],
        rows,
        rows * 2048,
    )[0]


def from_behind(block, axis, distance):
    devices = range(lax.axis_size(axis))
    route = [((i - distance) % len(devices), i) for i in devices]
    return lax.ppermute(block, axis, route)


def exchange(blocks):
    count, width = blocks.shape
    members = lax.axis_size("lat") * lax.axis_size("lon")
    split = blocks.reshape(members, count // members, width)
    moved = lax.all_to_all(split, ("lat", "lon"), split_axis=0, concat_axis=0, tiled=True)
    return moved.reshape(count, width)


def local(
    tokens,
    pad_rows,
    land_sea,
    win_gain,
    win_query,
    win_key,
    win_value,
    win_out,
    grid_gain,
    grid_query,
    grid_key,
    grid_value,
    grid_out,
):
    height, breadth, width = tokens.shape
    flat = tokens.reshape(height * breadth, width)
    pads = pad_rows.reshape(1, -1)
    halo = from_behind(tokens[:, :SHIFT].reshape(height * SHIFT, width), "lon", -1)
    win_weights = (win_query, win_key, win_value, win_out)
    grid_weights = (grid_query, grid_key, grid_value, grid_out)
    blocks, *held = window_part(
        flat, halo, pads, land_sea, win_gain.reshape(1, -1), win_weights, grid_weights
    )
    mixed = exchange(grid_part(exchange(blocks), pads, grid_gain.reshape(1, -1), held))
    halves = mixed.reshape(height * breadth // 4, 2, 4, width // 2)
    return halves.transpose(0, 2, 1, 3).reshape(height, breadth, width)


def solution(mesh):
    whole = P()
    split = P("lat", "lon", None)
    placed = (split, whole, split) + (whole,) * 10
    return jax.shard_map(local, mesh=mesh, in_specs=placed, out_specs=split, check_vma=False)
```

```python
import functools
import math

import jax
import jax.numpy as jnp
from jax import lax
from jax.experimental import pallas as pl
from jax.experimental.pallas import tpu as pltpu
from jax.sharding import PartitionSpec as P

HEADS = 16
GROUPS = 4
WIN = 8
SHIFT = 4
EPSILON = 1e-06
MASKED = -1e30
BF16 = jnp.bfloat16
F32 = jnp.float32
I32 = jnp.int32


def iota(shape, axis):
    return lax.broadcasted_iota(I32, shape, axis)


def one_hot(hits):
    return jnp.where(hits, 1.0, 0.0).astype(BF16)


def matmul(left, right):
    return jnp.dot(left, right, preferred_element_type=F32)


def matmul_nt(left, right):
    return lax.dot_general(left, right, (((1,), (1,)), ((), ())), preferred_element_type=F32)


def norm(rows, gain):
    mean_sq = jnp.mean(rows * rows, axis=-1, keepdims=True)
    return (rows * lax.rsqrt(mean_sq + EPSILON) * gain).astype(BF16)


def usable_bias(pad_ref, wanted_row):
    lanes = wanted_row.shape[1]
    pads = jnp.broadcast_to(pad_ref[...].astype(F32).astype(BF16), (16, pad_ref.shape[1]))
    picks = one_hot(iota((pad_ref.shape[1], lanes), 0) == wanted_row)
    return jnp.where(matmul(pads, picks)[:1] > 0.5, 0.0, MASKED)


def fetch(pairs, sems):
    copies = [
        pltpu.make_async_copy(source, target, sems.at[n]) for n, (source, target) in enumerate(pairs)
    ]
    for copy in copies:
        copy.start()
    return copies


def cross(upper, lower):
    first = iota((1, 8, 1), 1) < 4
    return (
        jnp.where(first, upper, jnp.roll(lower, 4, axis=1)),
        jnp.where(first, jnp.roll(upper, 4, axis=1), lower),
    )


def block_tiles(tiles):
    half = tiles.shape[2] // 2
    return jnp.stack(cross(tiles[:, :, :half], tiles[:, :, half:]), axis=1)


def project(rows, weight, target_ref, factor=None):
    product = matmul(rows, weight[...])
    if factor is not None:
        product = product * factor
    target_ref[...] = product.astype(BF16)


def query_factor(head_size):
    return math.log2(math.e) / math.sqrt(head_size)


def window_attention(bands, gate_of, pad_ref, q_ref, k_ref, v_ref, heads_ref):
    width = q_ref.shape[1]
    head_size = width // HEADS
    quad = 4 * head_size
    first = lax.axis_index("lat") * 16
    key_lane = iota((1, quad), 1) % 64
    biases = [usable_bias(pad_ref, first + band * 8 + key_lane // 8) for band in range(2)]
    head_lane = iota((1, quad), 1) // head_size
    masks = [one_hot(head_lane == h) for h in range(4)]
    ones = one_hot(iota((quad, quad), 0) // 64 == iota((quad, quad), 1) // head_size)
    lower = iota((1, 128), 1) < 64

    def spread(block):
        return jnp.concatenate([block * mask for mask in masks], axis=0)

    for tile, band in enumerate(bands):
        span = slice(tile * 64, (tile + 1) * 64)
        for group in range(GROUPS):
            lanes = slice(group * quad, (group + 1) * quad)
            scores = matmul_nt(q_ref[span, lanes], spread(k_ref[span, lanes])) + biases[band]
            exps = []
            for block in range(2):
                part_scores = scores[:, block * 128 : (block + 1) * 128]
                low = jnp.max(jnp.where(lower, part_scores, -jnp.inf), axis=1, keepdims=True)
                high = jnp.max(jnp.where(lower, -jnp.inf, part_scores), axis=1, keepdims=True)
                exps.append(jnp.exp2(part_scores - jnp.where(lower, low, high)).astype(BF16))
            weight = jnp.concatenate(exps, axis=1)
            total = matmul(weight, ones)
            heads = matmul(weight, spread(v_ref[span, lanes])) / total * gate_of(tile, group)
            heads_ref[span, lanes] = heads.astype(BF16)


def swap_halves(tiles):
    return jnp.roll(tiles, 4, axis=1)


def project_kernel(
    tok_hbm, land_hbm, pad_hbm, gain_hbm, grid_gain_hbm, wq_hbm, wk_hbm, wv_hbm,
    halo_ref, x_ref, edge_ref, gate_ref, pad_ref, gain_ref, grid_gain_ref, wq_ref, wk_ref, wv_ref,
    normed_ref, q_ref,
    tok_ref, land_ref, sems,
):
    copies = fetch(
        [
            (tok_hbm, tok_ref), (land_hbm, land_ref), (gain_hbm, gain_ref),
            (pad_hbm, pad_ref), (grid_gain_hbm, grid_gain_ref),
            (wq_hbm, wq_ref), (wk_hbm, wk_ref), (wv_hbm, wv_ref),
        ],
        sems,
    )
    cells, width = tok_ref.shape
    rows = q_ref.shape[0]
    for copy in copies[:5]:
        copy.wait()
    tiles = tok_ref[...].astype(F32).reshape(16, 4, 8, width)
    first = iota((1, 8, 1), 1) < 4
    pairs = tiles[:, 3].reshape(8, 2, 8, width)
    halo = jnp.where(first, swap_halves(pairs[:, 0]), pairs[:, 1])
    halo_ref[0:64, :] = halo.reshape(64, width).astype(BF16)
    tile_at, group_at = iota((8, width), 0), iota((8, width), 1) // (width // GROUPS)
    gates = jnp.zeros((8, width), F32)
    for tile in range(8):
        for n in range(GROUPS):
            gate = land_ref[tile // 4, tile % 4, n].astype(F32)
            gates = jnp.where((tile_at == tile) & (group_at == n), gate, gates)
    gate_ref[...] = gates
    outer_gates = [gates[3:4], gates[7:8], jnp.zeros((14, width), F32)]
    halo_ref[64:80, :] = jnp.concatenate(outer_gates, axis=0).astype(BF16)
    edge_ref[...] = tiles[:, 0].reshape(128, width).astype(BF16)
    pieces = []
    for band in range(2):
        lines = slice(band * 8, band * 8 + 8)
        for tile_col in range(3):
            pieces.append(
                swap_halves(jnp.where(first, tiles[lines, tile_col + 1], tiles[lines, tile_col]))
            )
    x = jnp.concatenate(pieces, axis=0).reshape(rows, width)
    x_ref[...] = x
    normed = norm(x, gain_ref[...])
    normed_ref[...] = normed
    copies[5].wait()
    project(normed, wq_ref, q_ref, query_factor(width // HEADS))
    for copy in copies[6:]:
        copy.wait()


def inner_kernel(
    x_ref, normed_ref, q_ref, wk_ref, wv_ref, pad_ref, gate_ref,
    wo_hbm, gq_hbm, gk_hbm, gv_hbm, go_hbm,
    out_ref, wo_ref, gq_ref, gk_ref, gv_ref, go_ref,
    k_ref, v_ref, heads_ref, sems,
):
    copies = fetch(
        [
            (wo_hbm, wo_ref), (gq_hbm, gq_ref), (gk_hbm, gk_ref), (gv_hbm, gv_ref),
            (go_hbm, go_ref),
        ],
        sems,
    )
    rows, width = heads_ref.shape
    quad = width // GROUPS
    normed = normed_ref[...]
    project(normed, wk_ref, k_ref)
    project(normed, wv_ref, v_ref)

    def gate_of(tile, group):
        row = tile // 3 * 4 + tile % 3
        return gate_ref[row : row + 1, group * quad : (group + 1) * quad]

    window_attention([0, 0, 0, 1, 1, 1], gate_of, pad_ref, q_ref, k_ref, v_ref, heads_ref)
    copies[0].wait()
    after = x_ref[...] + matmul(heads_ref[...], wo_ref[...])
    blocks = block_tiles(after.reshape(rows // 8, 8, width))
    out_ref[...] = blocks.reshape(2 * rows, width // 2).astype(BF16)
    for copy in copies[1:]:
        copy.wait()


def outer_kernel(
    inner_ref, halo_ref, edge_ref, gain_ref, wq_ref, wk_ref, wv_ref, wo_ref, pad_ref,
    out_ref, q_ref, k_ref, v_ref, heads_ref,
):
    rows, width = heads_ref.shape
    first = iota((1, 8, 1), 1) < 4
    own = edge_ref[...].astype(F32).reshape(8, 2, 8, width)
    halo = halo_ref[0:64, :].astype(F32).reshape(8, 8, width)
    even = jnp.where(first, halo, swap_halves(own[:, 0]))
    odd = swap_halves(jnp.where(first, own[:, 1], halo))
    gates = halo_ref[64:80, :].astype(F32)
    x = jnp.stack([even, odd], axis=1).reshape(rows, width)
    normed = norm(x, gain_ref[...])
    project(normed, wq_ref, q_ref, query_factor(width // HEADS))
    project(normed, wk_ref, k_ref)
    project(normed, wv_ref, v_ref)

    def gate_of(tile, group):
        return gates[tile : tile + 1, group * (width // GROUPS) : (group + 1) * (width // GROUPS)]

    window_attention([0, 1], gate_of, pad_ref, q_ref, k_ref, v_ref, heads_ref)
    after = x + matmul(heads_ref[...], wo_ref[...])
    outer = block_tiles(after.reshape(16, 8, width))
    inner = inner_ref[...].astype(F32).reshape(2, 3, 8, 2, 8, width // 2)
    for band in range(2):
        lines = slice(band * 8, band * 8 + 8)
        ordered = [outer[lines, 1]]
        for tile_col in range(3):
            ordered += [inner[band, tile_col, :, 0], inner[band, tile_col, :, 1]]
        ordered.append(outer[lines, 0])
        blocks = jnp.stack(ordered, axis=1).reshape(512, width // 2)
        out_ref[band * 512 : (band + 1) * 512, :] = blocks.astype(BF16)


def in_hbm(arrays):
    return [pltpu.with_memory_space_constraint(a, pltpu.HBM) for a in arrays]


VMEM_SPEC = pl.BlockSpec(memory_space=pltpu.VMEM)
HBM_SPEC = pl.BlockSpec(memory_space=pltpu.HBM)


def call(kernel, name, outs, in_vmem, from_hbm, scratch, rows, exps):
    width = 1024
    return pl.pallas_call(
        kernel,
        out_shape=outs,
        in_specs=[VMEM_SPEC] * len(in_vmem) + [HBM_SPEC] * len(from_hbm),
        out_specs=[VMEM_SPEC] * len(outs),
        scratch_shapes=scratch,
        compiler_params=pltpu.CompilerParams(vmem_limit_bytes=28 * 2**20),
        cost_estimate=pl.CostEstimate(
            flops=8 * rows * width * width, bytes_accessed=10 * 2**20, transcendentals=exps
        ),
        name=name,
    )(*in_vmem, *in_hbm(from_hbm))


def window_part(tokens, pads, land_sea, gain, grid_gain, weights, grid_weights):
    cells, width = tokens.shape
    inner, outer = cells * 3 // 4, cells // 4
    weight = pltpu.VMEM((width, width), BF16)
    rows = pltpu.VMEM((inner, width), BF16)
    halo, x, edge, gates, pads_held, win_gain, gain_held, wq, wk, wv, normed, q = call(
        project_kernel,
        "window_project",
        [
            jax.ShapeDtypeStruct((cells // 8 + 16, width), BF16),
            pltpu.VMEM((inner, width), F32),
            pltpu.VMEM((outer, width), BF16),
            pltpu.VMEM((8, width), F32),
            pltpu.VMEM(pads.shape, I32),
            pltpu.VMEM(gain.shape, F32),
            pltpu.VMEM(grid_gain.shape, F32),
        ]
        + [weight] * 3
        + [rows] * 2,
        [],
        [tokens, land_sea, pads, gain, grid_gain, *weights[:3]],
        [
            pltpu.VMEM((cells, width), BF16),
            pltpu.SMEM(land_sea.shape, I32),
            pltpu.SemaphoreType.DMA((8,)),
        ],
        inner,
        0,
    )
    halo = from_behind(halo, "lon", 1)
    inside, wo, *grid_held = call(
        inner_kernel,
        "window_inner",
        [pltpu.VMEM((2 * inner, width // 2), BF16)] + [weight] * 5,
        [x, normed, q, wk, wv, pads_held, gates],
        [weights[3], *grid_weights],
        [rows] * 3 + [pltpu.SemaphoreType.DMA((5,))],
        inner,
        inner * 1024,
    )
    blocks = call(
        outer_kernel,
        "window_outer",
        [jax.ShapeDtypeStruct((2 * cells, width // 2), BF16)],
        [inside, halo, edge, win_gain, wq, wk, wv, wo, pads_held],
        [],
        [pltpu.VMEM((outer, width), BF16)] * 4,
        outer,
        outer * 1024,
    )[0]
    grid_held = [pads_held, gain_held, *grid_held]
    return blocks, grid_held


def grid_kernel(
    block_ref, pad_ref, gain_ref, wq_ref, wk_ref, wv_ref, wo_ref,
    out_ref, wide_ref, x_ref, normed_ref, q_ref, k_ref, v_ref, heads_ref,
):
    rows, width = q_ref.shape
    members = 128
    groups = rows // members
    head_size = width // HEADS
    pair = 2 * head_size
    chunks = wide_ref.shape[0]
    for chunk in range(chunks):
        wide_ref[chunk] = block_ref[:, chunk * 128 : (chunk + 1) * 128].astype(F32)
    lanes_of = [
        (slice(n * 128, (n + 1) * 128), n % chunks, n // chunks * groups)
        for n in range(2 * chunks)
    ]
    for group in range(groups):
        span = slice(group * members, (group + 1) * members)
        for lanes, chunk, start in lanes_of:
            x_ref[span, lanes] = wide_ref[chunk, pl.ds(start + group, members, stride=8), :]
        normed_ref[span, :] = norm(x_ref[span, :], gain_ref[...])
    normed = normed_ref[...]
    project(normed, wq_ref, q_ref, query_factor(head_size))
    project(normed, wk_ref, k_ref)
    project(normed, wv_ref, v_ref)
    key_lane = iota((1, 2 * members), 1) % members
    bias = usable_bias(pad_ref, (key_lane // 8) * 16 + lax.axis_index("lat"))
    masks = [one_hot(iota((1, pair), 1) // head_size == h) for h in range(2)]
    ones = one_hot(
        iota((2 * members, pair), 0) // members == iota((2 * members, pair), 1) // head_size
    )

    def spread(block):
        return jnp.concatenate([block * mask for mask in masks], axis=0)

    for group in range(groups):
        span = slice(group * members, (group + 1) * members)
        for two in range(HEADS // 2):
            lanes = slice(two * pair, (two + 1) * pair)
            scores = matmul_nt(q_ref[span, lanes], spread(k_ref[span, lanes])) + bias
            exps = []
            for half in range(2):
                head_scores = scores[:, half * members : (half + 1) * members]
                largest = jnp.max(head_scores, axis=1, keepdims=True)
                exps.append(jnp.exp2(head_scores - largest).astype(BF16))
            weight = jnp.concatenate(exps, axis=1)
            both = jnp.concatenate([spread(v_ref[span, lanes]), ones], axis=1)
            sums = matmul(weight, both)
            heads_ref[span, lanes] = (sums[:, :pair] / sums[:, pair:]).astype(BF16)
    wrapped = lax.axis_index("lon") == lax.axis_size("lon") - 1
    mixed = x_ref[...] + matmul(heads_ref[...], wo_ref[...])
    for group in range(groups):
        span = slice(group * members, (group + 1) * members)
        tiles = mixed[span].reshape(members // 8, 8, width)
        home = jnp.where(wrapped, jnp.roll(tiles, -1, axis=1), tiles).reshape(members, width)
        for lanes, chunk, start in lanes_of:
            wide_ref[chunk, pl.ds(start + group, members, stride=8), :] = home[:, lanes]
    for chunk in range(chunks):
        out_ref[:, chunk * 128 : (chunk + 1) * 128] = wide_ref[chunk].astype(BF16)


def grid_part(blocks, held):
    rows, width = blocks.shape[0] // 2, blocks.shape[1] * 2
    return call(
        grid_kernel,
        "grid_part",
        [jax.ShapeDtypeStruct(blocks.shape, BF16)],
        [blocks, *held],
        [],
        [
            pltpu.VMEM((blocks.shape[1] // 128, blocks.shape[0], 128), F32),
            pltpu.VMEM((rows, width), F32),
        ]
        + [pltpu.VMEM((rows, width), BF16)] * 5,
        rows,
        rows * 2048,
    )[0]


def final_kernel(block_ref, out_hbm, out_ref, sems):
    rows, width = out_ref.shape
    steps = 4
    part = rows // steps
    copies = []
    for step in range(steps):
        span = slice(step * part, (step + 1) * part)
        blocks = block_ref[2 * step * part : 2 * (step + 1) * part, :].astype(F32)
        tiles = blocks.reshape(part // 8, 2, 8, width // 2)
        whole = jnp.concatenate(cross(tiles[:, 0], tiles[:, 1]), axis=2)
        out_ref[span, :] = whole.reshape(part, width).astype(BF16)
        copy = pltpu.make_async_copy(out_ref.at[span], out_hbm.at[span], sems.at[step])
        copy.start()
        copies.append(copy)
    for copy in copies:
        copy.wait()


def final_part(blocks):
    rows, width = blocks.shape[0] // 2, blocks.shape[1] * 2
    return pl.pallas_call(
        final_kernel,
        out_shape=jax.ShapeDtypeStruct((rows, width), BF16),
        in_specs=[VMEM_SPEC],
        out_specs=HBM_SPEC,
        scratch_shapes=[pltpu.VMEM((rows, width), BF16), pltpu.SemaphoreType.DMA((4,))],
        compiler_params=pltpu.CompilerParams(vmem_limit_bytes=16 * 2**20),
        name="final_part",
    )(blocks)


def from_behind(block, axis, distance):
    devices = range(lax.axis_size(axis))
    route = [((i - distance) % len(devices), i) for i in devices]
    return lax.ppermute(block, axis, route)


def exchange(blocks):
    count, width = blocks.shape
    members = lax.axis_size("lat") * lax.axis_size("lon")
    split = blocks.reshape(members, count // members, width)
    moved = lax.all_to_all(split, ("lat", "lon"), split_axis=0, concat_axis=0, tiled=True)
    return moved.reshape(count, width)


def local(
    tokens,
    pad_rows,
    land_sea,
    win_gain,
    win_query,
    win_key,
    win_value,
    win_out,
    grid_gain,
    grid_query,
    grid_key,
    grid_value,
    grid_out,
):
    height, breadth, width = tokens.shape
    flat = tokens.reshape(height * breadth, width)
    pads = pad_rows.reshape(1, -1)
    win_weights = (win_query, win_key, win_value, win_out)
    grid_weights = (grid_query, grid_key, grid_value, grid_out)
    win_gain, grid_gain = win_gain.reshape(1, -1), grid_gain.reshape(1, -1)
    blocks, held = window_part(
        flat, pads, land_sea, win_gain, grid_gain, win_weights, grid_weights
    )
    mixed = exchange(grid_part(exchange(blocks), held))
    return final_part(mixed).reshape(height, breadth, width)


def solution(mesh):
    whole = P()
    split = P("lat", "lon", None)
    placed = (split, whole, split) + (whole,) * 10
    return jax.shard_map(local, mesh=mesh, in_specs=placed, out_specs=split, check_vma=False)
```

```python
import functools
import math

import jax
import jax.numpy as jnp
from jax import lax
from jax.experimental import pallas as pl
from jax.experimental.pallas import tpu as pltpu
from jax.sharding import PartitionSpec as P

HEADS = 16
GROUPS = 4
WIN = 8
SHIFT = 4
EPSILON = 1e-06
MASKED = -1e30
BF16 = jnp.bfloat16
F32 = jnp.float32
I32 = jnp.int32


def iota(shape, axis):
    return lax.broadcasted_iota(I32, shape, axis)


def one_hot(hits):
    return jnp.where(hits, 1.0, 0.0).astype(BF16)


def matmul(left, right):
    return jnp.dot(left, right, preferred_element_type=F32)


def matmul_nt(left, right):
    return lax.dot_general(left, right, (((1,), (1,)), ((), ())), preferred_element_type=F32)


def norm(rows, gain):
    mean_sq = jnp.mean(rows * rows, axis=-1, keepdims=True)
    return (rows * lax.rsqrt(mean_sq + EPSILON) * gain).astype(BF16)


def usable_bias(pad_ref, wanted_row):
    lanes = wanted_row.shape[1]
    pads = jnp.broadcast_to(pad_ref[...].astype(F32).astype(BF16), (16, pad_ref.shape[1]))
    picks = one_hot(iota((pad_ref.shape[1], lanes), 0) == wanted_row)
    return jnp.where(matmul(pads, picks)[:1] > 0.5, 0.0, MASKED)


def fetch(pairs, sems):
    copies = [
        pltpu.make_async_copy(source, target, sems.at[n]) for n, (source, target) in enumerate(pairs)
    ]
    for copy in copies:
        copy.start()
    return copies


def cross(upper, lower):
    first = iota((1, 8, 1), 1) < 4
    return (
        jnp.where(first, upper, jnp.roll(lower, 4, axis=1)),
        jnp.where(first, jnp.roll(upper, 4, axis=1), lower),
    )


def block_tiles(tiles):
    half = tiles.shape[2] // 2
    return jnp.stack(cross(tiles[:, :, :half], tiles[:, :, half:]), axis=1)


def project(rows, weight, target_ref, factor=None):
    product = matmul(rows, weight[...])
    if factor is not None:
        product = product * factor
    target_ref[...] = product.astype(BF16)


def query_factor(head_size):
    return math.log2(math.e) / math.sqrt(head_size)


def window_attention(bands, gate_of, pad_ref, q_ref, k_ref, v_ref, heads_ref):
    width = q_ref.shape[1]
    head_size = width // HEADS
    quad = 4 * head_size
    first = lax.axis_index("lat") * 16
    key_lane = iota((1, quad), 1) % 64
    biases = [usable_bias(pad_ref, first + band * 8 + key_lane // 8) for band in range(2)]
    head_lane = iota((1, quad), 1) // head_size
    masks = [one_hot(head_lane == h) for h in range(4)]
    ones = one_hot(iota((quad, quad), 0) // 64 == iota((quad, quad), 1) // head_size)
    lower = iota((1, 128), 1) < 64

    def spread(block):
        return jnp.concatenate([block * mask for mask in masks], axis=0)

    def weight_of(tile, group):
        span = slice(tile * 64, (tile + 1) * 64)
        lanes = slice(group * quad, (group + 1) * quad)
        scores = matmul_nt(q_ref[span, lanes], spread(k_ref[span, lanes])) + biases[bands[tile]]
        exps = []
        for block in range(2):
            part_scores = scores[:, block * 128 : (block + 1) * 128]
            low = jnp.max(jnp.where(lower, part_scores, -jnp.inf), axis=1, keepdims=True)
            high = jnp.max(jnp.where(lower, -jnp.inf, part_scores), axis=1, keepdims=True)
            exps.append(jnp.exp2(part_scores - jnp.where(lower, low, high)).astype(BF16))
        return jnp.concatenate(exps, axis=1)

    units = [(tile, group) for group in range(GROUPS) for tile in range(len(bands))]
    size = min(8, len(units))
    for start in range(0, len(units), size):
        batch = units[start : start + size]
        weights = [weight_of(*unit) for unit in batch]
        totals = matmul(jnp.concatenate(weights, axis=0), ones)
        for at, (tile, group) in enumerate(batch):
            span = slice(tile * 64, (tile + 1) * 64)
            lanes = slice(group * quad, (group + 1) * quad)
            total = totals[at * 64 : (at + 1) * 64]
            heads = matmul(weights[at], spread(v_ref[span, lanes])) / total * gate_of(tile, group)
            heads_ref[span, lanes] = heads.astype(BF16)


def swap_halves(tiles):
    return jnp.roll(tiles, 4, axis=1)


def project_kernel(
    tok_hbm, land_hbm, pad_hbm, gain_hbm, grid_gain_hbm, wq_hbm, wk_hbm, wv_hbm,
    halo_ref, x_ref, edge_ref, gate_ref, pad_ref, gain_ref, grid_gain_ref, wq_ref, wk_ref, wv_ref,
    normed_ref, q_ref,
    tok_ref, land_ref, sems,
):
    copies = fetch(
        [
            (tok_hbm, tok_ref), (land_hbm, land_ref), (gain_hbm, gain_ref),
            (pad_hbm, pad_ref), (grid_gain_hbm, grid_gain_ref),
            (wq_hbm, wq_ref), (wk_hbm, wk_ref), (wv_hbm, wv_ref),
        ],
        sems,
    )
    cells, width = tok_ref.shape
    rows = q_ref.shape[0]
    for copy in copies[:5]:
        copy.wait()
    tiles = tok_ref[...].astype(F32).reshape(16, 4, 8, width)
    first = iota((1, 8, 1), 1) < 4
    pairs = tiles[:, 3].reshape(8, 2, 8, width)
    halo = jnp.where(first, swap_halves(pairs[:, 0]), pairs[:, 1])
    halo_ref[0:64, :] = halo.reshape(64, width).astype(BF16)
    tile_at, group_at = iota((8, width), 0), iota((8, width), 1) // (width // GROUPS)
    gates = jnp.zeros((8, width), F32)
    for tile in range(8):
        for n in range(GROUPS):
            gate = land_ref[tile // 4, tile % 4, n].astype(F32)
            gates = jnp.where((tile_at == tile) & (group_at == n), gate, gates)
    gate_ref[...] = gates
    outer_gates = [gates[3:4], gates[7:8], jnp.zeros((14, width), F32)]
    halo_ref[64:80, :] = jnp.concatenate(outer_gates, axis=0).astype(BF16)
    edge_ref[...] = tiles[:, 0].reshape(128, width).astype(BF16)
    pieces = []
    for band in range(2):
        lines = slice(band * 8, band * 8 + 8)
        for tile_col in range(3):
            pieces.append(
                swap_halves(jnp.where(first, tiles[lines, tile_col + 1], tiles[lines, tile_col]))
            )
    x = jnp.concatenate(pieces, axis=0).reshape(rows, width)
    x_ref[...] = x
    normed = norm(x, gain_ref[...])
    normed_ref[...] = normed
    copies[5].wait()
    project(normed, wq_ref, q_ref, query_factor(width // HEADS))
    for copy in copies[6:]:
        copy.wait()


def inner_kernel(
    x_ref, normed_ref, q_ref, wk_ref, wv_ref, pad_ref, gate_ref,
    wo_hbm, gq_hbm, gk_hbm, gv_hbm, go_hbm,
    out_ref, wo_ref, gq_ref, gk_ref, gv_ref, go_ref,
    k_ref, v_ref, heads_ref, sems,
):
    copies = fetch(
        [
            (wo_hbm, wo_ref), (gq_hbm, gq_ref), (gk_hbm, gk_ref), (gv_hbm, gv_ref),
            (go_hbm, go_ref),
        ],
        sems,
    )
    rows, width = heads_ref.shape
    quad = width // GROUPS
    normed = normed_ref[...]
    project(normed, wk_ref, k_ref)
    project(normed, wv_ref, v_ref)

    def gate_of(tile, group):
        row = tile // 3 * 4 + tile % 3
        return gate_ref[row : row + 1, group * quad : (group + 1) * quad]

    window_attention([0, 0, 0, 1, 1, 1], gate_of, pad_ref, q_ref, k_ref, v_ref, heads_ref)
    copies[0].wait()
    after = x_ref[...] + matmul(heads_ref[...], wo_ref[...])
    blocks = block_tiles(after.reshape(rows // 8, 8, width))
    out_ref[...] = blocks.reshape(2 * rows, width // 2).astype(BF16)
    for copy in copies[1:]:
        copy.wait()


def outer_kernel(
    inner_ref, halo_ref, edge_ref, gain_ref, wq_ref, wk_ref, wv_ref, wo_ref, pad_ref,
    out_ref, q_ref, k_ref, v_ref, heads_ref,
):
    rows, width = heads_ref.shape
    first = iota((1, 8, 1), 1) < 4
    own = edge_ref[...].astype(F32).reshape(8, 2, 8, width)
    halo = halo_ref[0:64, :].astype(F32).reshape(8, 8, width)
    even = jnp.where(first, halo, swap_halves(own[:, 0]))
    odd = swap_halves(jnp.where(first, own[:, 1], halo))
    gates = halo_ref[64:80, :].astype(F32)
    x = jnp.stack([even, odd], axis=1).reshape(rows, width)
    normed = norm(x, gain_ref[...])
    project(normed, wq_ref, q_ref, query_factor(width // HEADS))
    project(normed, wk_ref, k_ref)
    project(normed, wv_ref, v_ref)

    def gate_of(tile, group):
        return gates[tile : tile + 1, group * (width // GROUPS) : (group + 1) * (width // GROUPS)]

    window_attention([0, 1], gate_of, pad_ref, q_ref, k_ref, v_ref, heads_ref)
    after = x + matmul(heads_ref[...], wo_ref[...])
    outer = block_tiles(after.reshape(16, 8, width))
    inner = inner_ref[...].astype(F32).reshape(2, 3, 8, 2, 8, width // 2)
    for band in range(2):
        lines = slice(band * 8, band * 8 + 8)
        ordered = [outer[lines, 1]]
        for tile_col in range(3):
            ordered += [inner[band, tile_col, :, 0], inner[band, tile_col, :, 1]]
        ordered.append(outer[lines, 0])
        blocks = jnp.stack(ordered, axis=1).reshape(512, width // 2)
        out_ref[band * 512 : (band + 1) * 512, :] = blocks.astype(BF16)


def in_hbm(arrays):
    return [pltpu.with_memory_space_constraint(a, pltpu.HBM) for a in arrays]


VMEM_SPEC = pl.BlockSpec(memory_space=pltpu.VMEM)
HBM_SPEC = pl.BlockSpec(memory_space=pltpu.HBM)


def call(kernel, name, outs, in_vmem, from_hbm, scratch, rows, exps):
    width = 1024
    return pl.pallas_call(
        kernel,
        out_shape=outs,
        in_specs=[VMEM_SPEC] * len(in_vmem) + [HBM_SPEC] * len(from_hbm),
        out_specs=[VMEM_SPEC] * len(outs),
        scratch_shapes=scratch,
        compiler_params=pltpu.CompilerParams(vmem_limit_bytes=28 * 2**20),
        cost_estimate=pl.CostEstimate(
            flops=8 * rows * width * width, bytes_accessed=10 * 2**20, transcendentals=exps
        ),
        name=name,
    )(*in_vmem, *in_hbm(from_hbm))


def window_part(tokens, pads, land_sea, gain, grid_gain, weights, grid_weights):
    cells, width = tokens.shape
    inner, outer = cells * 3 // 4, cells // 4
    weight = pltpu.VMEM((width, width), BF16)
    rows = pltpu.VMEM((inner, width), BF16)
    halo, x, edge, gates, pads_held, win_gain, gain_held, wq, wk, wv, normed, q = call(
        project_kernel,
        "window_project",
        [
            jax.ShapeDtypeStruct((cells // 8 + 16, width), BF16),
            pltpu.VMEM((inner, width), F32),
            pltpu.VMEM((outer, width), BF16),
            pltpu.VMEM((8, width), F32),
            pltpu.VMEM(pads.shape, I32),
            pltpu.VMEM(gain.shape, F32),
            pltpu.VMEM(grid_gain.shape, F32),
        ]
        + [weight] * 3
        + [rows] * 2,
        [],
        [tokens, land_sea, pads, gain, grid_gain, *weights[:3]],
        [
            pltpu.VMEM((cells, width), BF16),
            pltpu.SMEM(land_sea.shape, I32),
            pltpu.SemaphoreType.DMA((8,)),
        ],
        inner,
        0,
    )
    halo = from_behind(halo, "lon", 1)
    inside, wo, *grid_held = call(
        inner_kernel,
        "window_inner",
        [pltpu.VMEM((2 * inner, width // 2), BF16)] + [weight] * 5,
        [x, normed, q, wk, wv, pads_held, gates],
        [weights[3], *grid_weights],
        [rows] * 3 + [pltpu.SemaphoreType.DMA((5,))],
        inner,
        inner * 1024,
    )
    blocks = call(
        outer_kernel,
        "window_outer",
        [jax.ShapeDtypeStruct((2 * cells, width // 2), BF16)],
        [inside, halo, edge, win_gain, wq, wk, wv, wo, pads_held],
        [],
        [pltpu.VMEM((outer, width), BF16)] * 4,
        outer,
        outer * 1024,
    )[0]
    grid_held = [pads_held, gain_held, *grid_held]
    return blocks, grid_held


def grid_kernel(
    block_ref, pad_ref, gain_ref, wq_ref, wk_ref, wv_ref, wo_ref,
    out_ref, wide_ref, x_ref, normed_ref, q_ref, k_ref, v_ref, heads_ref,
):
    rows, width = q_ref.shape
    members = 128
    groups = rows // members
    head_size = width // HEADS
    pair = 2 * head_size
    chunks = wide_ref.shape[0]
    for chunk in range(chunks):
        wide_ref[chunk] = block_ref[:, chunk * 128 : (chunk + 1) * 128].astype(F32)
    lanes_of = [
        (slice(n * 128, (n + 1) * 128), n % chunks, n // chunks * groups)
        for n in range(2 * chunks)
    ]
    for group in range(groups):
        span = slice(group * members, (group + 1) * members)
        for lanes, chunk, start in lanes_of:
            x_ref[span, lanes] = wide_ref[chunk, pl.ds(start + group, members, stride=8), :]
        normed_ref[span, :] = norm(x_ref[span, :], gain_ref[...])
    normed = normed_ref[...]
    project(normed, wq_ref, q_ref, query_factor(head_size))
    project(normed, wk_ref, k_ref)
    project(normed, wv_ref, v_ref)
    key_lane = iota((1, 2 * members), 1) % members
    bias = usable_bias(pad_ref, (key_lane // 8) * 16 + lax.axis_index("lat"))
    masks = [one_hot(iota((1, pair), 1) // head_size == h) for h in range(2)]
    ones = one_hot(
        iota((2 * members, pair), 0) // members == iota((2 * members, pair), 1) // head_size
    )

    def spread(block):
        return jnp.concatenate([block * mask for mask in masks], axis=0)

    for group in range(groups):
        span = slice(group * members, (group + 1) * members)
        for two in range(HEADS // 2):
            lanes = slice(two * pair, (two + 1) * pair)
            scores = matmul_nt(q_ref[span, lanes], spread(k_ref[span, lanes])) + bias
            exps = []
            for half in range(2):
                head_scores = scores[:, half * members : (half + 1) * members]
                largest = jnp.max(head_scores, axis=1, keepdims=True)
                exps.append(jnp.exp2(head_scores - largest).astype(BF16))
            weight = jnp.concatenate(exps, axis=1)
            both = jnp.concatenate([spread(v_ref[span, lanes]), ones], axis=1)
            sums = matmul(weight, both)
            heads_ref[span, lanes] = (sums[:, :pair] / sums[:, pair:]).astype(BF16)
    wrapped = lax.axis_index("lon") == lax.axis_size("lon") - 1
    mixed = x_ref[...] + matmul(heads_ref[...], wo_ref[...])
    for group in range(groups):
        span = slice(group * members, (group + 1) * members)
        tiles = mixed[span].reshape(members // 8, 8, width)
        home = jnp.where(wrapped, jnp.roll(tiles, -1, axis=1), tiles).reshape(members, width)
        for lanes, chunk, start in lanes_of:
            wide_ref[chunk, pl.ds(start + group, members, stride=8), :] = home[:, lanes]
    for chunk in range(chunks):
        out_ref[:, chunk * 128 : (chunk + 1) * 128] = wide_ref[chunk].astype(BF16)


def grid_part(blocks, held):
    rows, width = blocks.shape[0] // 2, blocks.shape[1] * 2
    return call(
        grid_kernel,
        "grid_part",
        [jax.ShapeDtypeStruct(blocks.shape, BF16)],
        [blocks, *held],
        [],
        [
            pltpu.VMEM((blocks.shape[1] // 128, blocks.shape[0], 128), F32),
            pltpu.VMEM((rows, width), F32),
        ]
        + [pltpu.VMEM((rows, width), BF16)] * 5,
        rows,
        rows * 2048,
    )[0]


def final_kernel(block_ref, out_hbm, out_ref, sems):
    rows, width = out_ref.shape
    steps = 4
    part = rows // steps
    copies = []
    for step in range(steps):
        span = slice(step * part, (step + 1) * part)
        blocks = block_ref[2 * step * part : 2 * (step + 1) * part, :].astype(F32)
        tiles = blocks.reshape(part // 8, 2, 8, width // 2)
        whole = jnp.concatenate(cross(tiles[:, 0], tiles[:, 1]), axis=2)
        out_ref[span, :] = whole.reshape(part, width).astype(BF16)
        copy = pltpu.make_async_copy(out_ref.at[span], out_hbm.at[span], sems.at[step])
        copy.start()
        copies.append(copy)
    for copy in copies:
        copy.wait()


def final_part(blocks):
    rows, width = blocks.shape[0] // 2, blocks.shape[1] * 2
    return pl.pallas_call(
        final_kernel,
        out_shape=jax.ShapeDtypeStruct((rows, width), BF16),
        in_specs=[VMEM_SPEC],
        out_specs=HBM_SPEC,
        scratch_shapes=[pltpu.VMEM((rows, width), BF16), pltpu.SemaphoreType.DMA((4,))],
        compiler_params=pltpu.CompilerParams(vmem_limit_bytes=16 * 2**20),
        name="final_part",
    )(blocks)


def from_behind(block, axis, distance):
    devices = range(lax.axis_size(axis))
    route = [((i - distance) % len(devices), i) for i in devices]
    return lax.ppermute(block, axis, route)


def exchange(blocks):
    count, width = blocks.shape
    members = lax.axis_size("lat") * lax.axis_size("lon")
    split = blocks.reshape(members, count // members, width)
    moved = lax.all_to_all(split, ("lat", "lon"), split_axis=0, concat_axis=0, tiled=True)
    return moved.reshape(count, width)


def local(
    tokens,
    pad_rows,
    land_sea,
    win_gain,
    win_query,
    win_key,
    win_value,
    win_out,
    grid_gain,
    grid_query,
    grid_key,
    grid_value,
    grid_out,
):
    height, breadth, width = tokens.shape
    flat = tokens.reshape(height * breadth, width)
    pads = pad_rows.reshape(1, -1)
    win_weights = (win_query, win_key, win_value, win_out)
    grid_weights = (grid_query, grid_key, grid_value, grid_out)
    win_gain, grid_gain = win_gain.reshape(1, -1), grid_gain.reshape(1, -1)
    blocks, held = window_part(
        flat, pads, land_sea, win_gain, grid_gain, win_weights, grid_weights
    )
    mixed = exchange(grid_part(exchange(blocks), held))
    return final_part(mixed).reshape(height, breadth, width)


def solution(mesh):
    whole = P()
    split = P("lat", "lon", None)
    placed = (split, whole, split) + (whole,) * 10
    return jax.shard_map(local, mesh=mesh, in_specs=placed, out_specs=split, check_vma=False)
```

```python
import functools
import math

import jax
import jax.numpy as jnp
from jax import lax
from jax.experimental import pallas as pl
from jax.experimental.pallas import tpu as pltpu
from jax.sharding import PartitionSpec as P

HEADS = 16
GROUPS = 4
WIN = 8
SHIFT = 4
EPSILON = 1e-06
MASKED = -1e30
BF16 = jnp.bfloat16
F32 = jnp.float32
I32 = jnp.int32


def iota(shape, axis):
    return lax.broadcasted_iota(I32, shape, axis)


def one_hot(hits):
    return jnp.where(hits, 1.0, 0.0).astype(BF16)


def matmul(left, right):
    return jnp.dot(left, right, preferred_element_type=F32)


def matmul_nt(left, right):
    return lax.dot_general(left, right, (((1,), (1,)), ((), ())), preferred_element_type=F32)


def norm(rows, gain):
    mean_sq = jnp.mean(rows * rows, axis=-1, keepdims=True)
    return (rows * lax.rsqrt(mean_sq + EPSILON) * gain).astype(BF16)


def usable_bias(pad_ref, wanted_row):
    lanes = wanted_row.shape[1]
    pads = jnp.broadcast_to(pad_ref[...].astype(F32).astype(BF16), (16, pad_ref.shape[1]))
    picks = one_hot(iota((pad_ref.shape[1], lanes), 0) == wanted_row)
    return jnp.where(matmul(pads, picks)[:1] > 0.5, 0.0, MASKED)


def fetch(pairs, sems):
    copies = [
        pltpu.make_async_copy(source, target, sems.at[n]) for n, (source, target) in enumerate(pairs)
    ]
    for copy in copies:
        copy.start()
    return copies


def cross(upper, lower):
    first = iota((1, 8, 1), 1) < 4
    return (
        jnp.where(first, upper, jnp.roll(lower, 4, axis=1)),
        jnp.where(first, jnp.roll(upper, 4, axis=1), lower),
    )


def block_tiles(tiles):
    half = tiles.shape[2] // 2
    return jnp.stack(cross(tiles[:, :, :half], tiles[:, :, half:]), axis=1)


def project(rows, weight, target_ref, factor=None):
    product = matmul(rows, weight[...])
    if factor is not None:
        product = product * factor
    target_ref[...] = product.astype(BF16)


def query_factor(head_size):
    return math.log2(math.e) / math.sqrt(head_size)


def window_attention(bands, gate_of, pad_ref, q_ref, k_ref, v_ref, heads_ref):
    width = q_ref.shape[1]
    head_size = width // HEADS
    quad = 4 * head_size
    first = lax.axis_index("lat") * 16
    key_lane = iota((1, quad), 1) % 64
    biases = [usable_bias(pad_ref, first + band * 8 + key_lane // 8) for band in range(2)]
    head_lane = iota((1, quad), 1) // head_size
    masks = [one_hot(head_lane == h) for h in range(4)]
    ones = one_hot(iota((quad, quad), 0) // 64 == iota((quad, quad), 1) // head_size)
    lower = iota((1, 128), 1) < 64

    def spread(block):
        return jnp.concatenate([block * mask for mask in masks], axis=0)

    def weight_of(tile, group):
        span = slice(tile * 64, (tile + 1) * 64)
        lanes = slice(group * quad, (group + 1) * quad)
        scores = matmul_nt(q_ref[span, lanes], spread(k_ref[span, lanes])) + biases[bands[tile]]
        exps = []
        for block in range(2):
            part_scores = scores[:, block * 128 : (block + 1) * 128]
            low = jnp.max(jnp.where(lower, part_scores, -jnp.inf), axis=1, keepdims=True)
            high = jnp.max(jnp.where(lower, -jnp.inf, part_scores), axis=1, keepdims=True)
            exps.append(jnp.exp2(part_scores - jnp.where(lower, low, high)).astype(BF16))
        return jnp.concatenate(exps, axis=1)

    units = [(tile, group) for group in range(GROUPS) for tile in range(len(bands))]
    batches = [units[at : at + 4] for at in range(0, len(units), 4)]

    def finish(batch, weights):
        totals = matmul(jnp.concatenate(weights, axis=0), ones)
        for at, (tile, group) in enumerate(batch):
            span = slice(tile * 64, (tile + 1) * 64)
            lanes = slice(group * quad, (group + 1) * quad)
            total = totals[at * 64 : (at + 1) * 64]
            heads = matmul(weights[at], spread(v_ref[span, lanes])) / total * gate_of(tile, group)
            heads_ref[span, lanes] = heads.astype(BF16)

    last = None
    for batch in batches:
        weights = [weight_of(*unit) for unit in batch]
        if last is not None:
            finish(*last)
        last = (batch, weights)
    finish(*last)


def swap_halves(tiles):
    return jnp.roll(tiles, 4, axis=1)


def project_kernel(
    tok_hbm, land_hbm, pad_hbm, gain_hbm, grid_gain_hbm, wq_hbm, wk_hbm, wv_hbm,
    halo_ref, x_ref, edge_ref, gate_ref, pad_ref, gain_ref, grid_gain_ref, wq_ref, wk_ref, wv_ref,
    normed_ref, q_ref,
    tok_ref, land_ref, sems,
):
    copies = fetch(
        [
            (tok_hbm, tok_ref), (land_hbm, land_ref), (gain_hbm, gain_ref),
            (pad_hbm, pad_ref), (grid_gain_hbm, grid_gain_ref),
            (wq_hbm, wq_ref), (wk_hbm, wk_ref), (wv_hbm, wv_ref),
        ],
        sems,
    )
    cells, width = tok_ref.shape
    rows = q_ref.shape[0]
    for copy in copies[:5]:
        copy.wait()
    tiles = tok_ref[...].astype(F32).reshape(16, 4, 8, width)
    first = iota((1, 8, 1), 1) < 4
    pairs = tiles[:, 3].reshape(8, 2, 8, width)
    halo = jnp.where(first, swap_halves(pairs[:, 0]), pairs[:, 1])
    halo_ref[0:64, :] = halo.reshape(64, width).astype(BF16)
    tile_at, group_at = iota((8, width), 0), iota((8, width), 1) // (width // GROUPS)
    gates = jnp.zeros((8, width), F32)
    for tile in range(8):
        for n in range(GROUPS):
            gate = land_ref[tile // 4, tile % 4, n].astype(F32)
            gates = jnp.where((tile_at == tile) & (group_at == n), gate, gates)
    gate_ref[...] = gates
    outer_gates = [gates[3:4], gates[7:8], jnp.zeros((14, width), F32)]
    halo_ref[64:80, :] = jnp.concatenate(outer_gates, axis=0).astype(BF16)
    edge_ref[...] = tiles[:, 0].reshape(128, width).astype(BF16)
    pieces = []
    for band in range(2):
        lines = slice(band * 8, band * 8 + 8)
        for tile_col in range(3):
            pieces.append(
                swap_halves(jnp.where(first, tiles[lines, tile_col + 1], tiles[lines, tile_col]))
            )
    x = jnp.concatenate(pieces, axis=0).reshape(rows, width)
    x_ref[...] = x
    normed = norm(x, gain_ref[...])
    normed_ref[...] = normed
    copies[5].wait()
    project(normed, wq_ref, q_ref, query_factor(width // HEADS))
    for copy in copies[6:]:
        copy.wait()


def inner_kernel(
    x_ref, normed_ref, q_ref, wk_ref, wv_ref, pad_ref, gate_ref,
    wo_hbm, gq_hbm, gk_hbm, gv_hbm, go_hbm,
    out_ref, wo_ref, gq_ref, gk_ref, gv_ref, go_ref,
    k_ref, v_ref, heads_ref, sems,
):
    copies = fetch(
        [
            (wo_hbm, wo_ref), (gq_hbm, gq_ref), (gk_hbm, gk_ref), (gv_hbm, gv_ref),
            (go_hbm, go_ref),
        ],
        sems,
    )
    rows, width = heads_ref.shape
    quad = width // GROUPS
    normed = normed_ref[...]
    project(normed, wk_ref, k_ref)
    project(normed, wv_ref, v_ref)

    def gate_of(tile, group):
        row = tile // 3 * 4 + tile % 3
        return gate_ref[row : row + 1, group * quad : (group + 1) * quad]

    window_attention([0, 0, 0, 1, 1, 1], gate_of, pad_ref, q_ref, k_ref, v_ref, heads_ref)
    copies[0].wait()
    after = x_ref[...] + matmul(heads_ref[...], wo_ref[...])
    blocks = block_tiles(after.reshape(rows // 8, 8, width))
    out_ref[...] = blocks.reshape(2 * rows, width // 2).astype(BF16)
    for copy in copies[1:]:
        copy.wait()


def outer_kernel(
    inner_ref, halo_ref, edge_ref, gain_ref, wq_ref, wk_ref, wv_ref, wo_ref, pad_ref,
    out_ref, q_ref, k_ref, v_ref, heads_ref,
):
    rows, width = heads_ref.shape
    first = iota((1, 8, 1), 1) < 4
    own = edge_ref[...].astype(F32).reshape(8, 2, 8, width)
    halo = halo_ref[0:64, :].astype(F32).reshape(8, 8, width)
    even = jnp.where(first, halo, swap_halves(own[:, 0]))
    odd = swap_halves(jnp.where(first, own[:, 1], halo))
    gates = halo_ref[64:80, :].astype(F32)
    x = jnp.stack([even, odd], axis=1).reshape(rows, width)
    normed = norm(x, gain_ref[...])
    project(normed, wq_ref, q_ref, query_factor(width // HEADS))
    project(normed, wk_ref, k_ref)
    project(normed, wv_ref, v_ref)

    def gate_of(tile, group):
        return gates[tile : tile + 1, group * (width // GROUPS) : (group + 1) * (width // GROUPS)]

    window_attention([0, 1], gate_of, pad_ref, q_ref, k_ref, v_ref, heads_ref)
    after = x + matmul(heads_ref[...], wo_ref[...])
    outer = block_tiles(after.reshape(16, 8, width))
    inner = inner_ref[...].astype(F32).reshape(2, 3, 8, 2, 8, width // 2)
    for band in range(2):
        lines = slice(band * 8, band * 8 + 8)
        ordered = [outer[lines, 1]]
        for tile_col in range(3):
            ordered += [inner[band, tile_col, :, 0], inner[band, tile_col, :, 1]]
        ordered.append(outer[lines, 0])
        blocks = jnp.stack(ordered, axis=1).reshape(512, width // 2)
        out_ref[band * 512 : (band + 1) * 512, :] = blocks.astype(BF16)


def in_hbm(arrays):
    return [pltpu.with_memory_space_constraint(a, pltpu.HBM) for a in arrays]


VMEM_SPEC = pl.BlockSpec(memory_space=pltpu.VMEM)
HBM_SPEC = pl.BlockSpec(memory_space=pltpu.HBM)


def call(kernel, name, outs, in_vmem, from_hbm, scratch, rows, exps):
    width = 1024
    return pl.pallas_call(
        kernel,
        out_shape=outs,
        in_specs=[VMEM_SPEC] * len(in_vmem) + [HBM_SPEC] * len(from_hbm),
        out_specs=[VMEM_SPEC] * len(outs),
        scratch_shapes=scratch,
        compiler_params=pltpu.CompilerParams(vmem_limit_bytes=28 * 2**20),
        cost_estimate=pl.CostEstimate(
            flops=8 * rows * width * width, bytes_accessed=10 * 2**20, transcendentals=exps
        ),
        name=name,
    )(*in_vmem, *in_hbm(from_hbm))


def window_part(tokens, pads, land_sea, gain, grid_gain, weights, grid_weights):
    cells, width = tokens.shape
    inner, outer = cells * 3 // 4, cells // 4
    weight = pltpu.VMEM((width, width), BF16)
    rows = pltpu.VMEM((inner, width), BF16)
    halo, x, edge, gates, pads_held, win_gain, gain_held, wq, wk, wv, normed, q = call(
        project_kernel,
        "window_project",
        [
            jax.ShapeDtypeStruct((cells // 8 + 16, width), BF16),
            pltpu.VMEM((inner, width), F32),
            pltpu.VMEM((outer, width), BF16),
            pltpu.VMEM((8, width), F32),
            pltpu.VMEM(pads.shape, I32),
            pltpu.VMEM(gain.shape, F32),
            pltpu.VMEM(grid_gain.shape, F32),
        ]
        + [weight] * 3
        + [rows] * 2,
        [],
        [tokens, land_sea, pads, gain, grid_gain, *weights[:3]],
        [
            pltpu.VMEM((cells, width), BF16),
            pltpu.SMEM(land_sea.shape, I32),
            pltpu.SemaphoreType.DMA((8,)),
        ],
        inner,
        0,
    )
    halo = from_behind(halo, "lon", 1)
    inside, wo, *grid_held = call(
        inner_kernel,
        "window_inner",
        [pltpu.VMEM((2 * inner, width // 2), BF16)] + [weight] * 5,
        [x, normed, q, wk, wv, pads_held, gates],
        [weights[3], *grid_weights],
        [rows] * 3 + [pltpu.SemaphoreType.DMA((5,))],
        inner,
        inner * 1024,
    )
    blocks = call(
        outer_kernel,
        "window_outer",
        [jax.ShapeDtypeStruct((2 * cells, width // 2), BF16)],
        [inside, halo, edge, win_gain, wq, wk, wv, wo, pads_held],
        [],
        [pltpu.VMEM((outer, width), BF16)] * 4,
        outer,
        outer * 1024,
    )[0]
    grid_held = [pads_held, gain_held, *grid_held]
    return blocks, grid_held


def grid_kernel(
    block_ref, pad_ref, gain_ref, wq_ref, wk_ref, wv_ref, wo_ref,
    out_ref, wide_ref, x_ref, normed_ref, q_ref, k_ref, v_ref, heads_ref,
):
    rows, width = q_ref.shape
    members = 128
    groups = rows // members
    head_size = width // HEADS
    pair = 2 * head_size
    chunks = wide_ref.shape[0]
    for chunk in range(chunks):
        wide_ref[chunk, : 2 * rows] = block_ref[:, chunk * 128 : (chunk + 1) * 128].astype(F32)
    lanes_of = [
        (slice(n * 128, (n + 1) * 128), n % chunks, n // chunks * groups)
        for n in range(2 * chunks)
    ]
    for group in range(groups):
        span = slice(group * members, (group + 1) * members)
        for lanes, chunk, start in lanes_of:
            x_ref[span, lanes] = wide_ref[chunk, pl.ds(start + group, members, stride=8), :]
        normed_ref[span, :] = norm(x_ref[span, :], gain_ref[...])
    normed = normed_ref[...]
    project(normed, wq_ref, q_ref, query_factor(head_size))
    project(normed, wk_ref, k_ref)
    project(normed, wv_ref, v_ref)
    key_lane = iota((1, 2 * members), 1) % members
    bias = usable_bias(pad_ref, (key_lane // 8) * 16 + lax.axis_index("lat"))
    masks = [one_hot(iota((1, pair), 1) // head_size == h) for h in range(2)]
    ones = one_hot(
        iota((2 * members, pair), 0) // members == iota((2 * members, pair), 1) // head_size
    )

    def spread(block):
        return jnp.concatenate([block * mask for mask in masks], axis=0)

    for group in range(groups):
        span = slice(group * members, (group + 1) * members)
        for two in range(HEADS // 2):
            lanes = slice(two * pair, (two + 1) * pair)
            scores = matmul_nt(q_ref[span, lanes], spread(k_ref[span, lanes])) + bias
            exps = []
            for half in range(2):
                head_scores = scores[:, half * members : (half + 1) * members]
                largest = jnp.max(head_scores, axis=1, keepdims=True)
                exps.append(jnp.exp2(head_scores - largest).astype(BF16))
            weight = jnp.concatenate(exps, axis=1)
            both = jnp.concatenate([spread(v_ref[span, lanes]), ones], axis=1)
            sums = matmul(weight, both)
            heads_ref[span, lanes] = (sums[:, :pair] / sums[:, pair:]).astype(BF16)
    wrapped = lax.axis_index("lon") == lax.axis_size("lon") - 1
    mixed = x_ref[...] + matmul(heads_ref[...], wo_ref[...])
    for group in range(groups):
        span = slice(group * members, (group + 1) * members)
        tiles = mixed[span].reshape(members // 8, 8, width)
        home = jnp.where(wrapped, jnp.roll(tiles, -1, axis=1), tiles).reshape(members, width)
        for lanes, chunk, start in lanes_of:
            wide_ref[chunk, pl.ds(start + group, members, stride=8), :] = home[:, lanes]
    for chunk in range(chunks):
        out_ref[:, chunk * 128 : (chunk + 1) * 128] = wide_ref[chunk, : 2 * rows].astype(BF16)


def grid_part(blocks, held):
    rows, width = blocks.shape[0] // 2, blocks.shape[1] * 2
    return call(
        grid_kernel,
        "grid_part",
        [jax.ShapeDtypeStruct(blocks.shape, BF16)],
        [blocks, *held],
        [],
        [
            pltpu.VMEM((blocks.shape[1] // 128, blocks.shape[0] + 8, 128), F32),
            pltpu.VMEM((rows, width), F32),
        ]
        + [pltpu.VMEM((rows, width), BF16)] * 5,
        rows,
        rows * 2048,
    )[0]


def final_kernel(block_ref, out_hbm, out_ref, sems):
    rows, width = out_ref.shape
    steps = 4
    part = rows // steps
    copies = []
    for step in range(steps):
        span = slice(step * part, (step + 1) * part)
        blocks = block_ref[2 * step * part : 2 * (step + 1) * part, :].astype(F32)
        tiles = blocks.reshape(part // 8, 2, 8, width // 2)
        whole = jnp.concatenate(cross(tiles[:, 0], tiles[:, 1]), axis=2)
        out_ref[span, :] = whole.reshape(part, width).astype(BF16)
        copy = pltpu.make_async_copy(out_ref.at[span], out_hbm.at[span], sems.at[step])
        copy.start()
        copies.append(copy)
    for copy in copies:
        copy.wait()


def final_part(blocks):
    rows, width = blocks.shape[0] // 2, blocks.shape[1] * 2
    return pl.pallas_call(
        final_kernel,
        out_shape=jax.ShapeDtypeStruct((rows, width), BF16),
        in_specs=[VMEM_SPEC],
        out_specs=HBM_SPEC,
        scratch_shapes=[pltpu.VMEM((rows, width), BF16), pltpu.SemaphoreType.DMA((4,))],
        compiler_params=pltpu.CompilerParams(vmem_limit_bytes=16 * 2**20),
        name="final_part",
    )(blocks)


def from_behind(block, axis, distance):
    devices = range(lax.axis_size(axis))
    route = [((i - distance) % len(devices), i) for i in devices]
    return lax.ppermute(block, axis, route)


def exchange(blocks):
    count, width = blocks.shape
    members = lax.axis_size("lat") * lax.axis_size("lon")
    split = blocks.reshape(members, count // members, width)
    moved = lax.all_to_all(split, ("lat", "lon"), split_axis=0, concat_axis=0, tiled=True)
    return moved.reshape(count, width)


def local(
    tokens,
    pad_rows,
    land_sea,
    win_gain,
    win_query,
    win_key,
    win_value,
    win_out,
    grid_gain,
    grid_query,
    grid_key,
    grid_value,
    grid_out,
):
    height, breadth, width = tokens.shape
    flat = tokens.reshape(height * breadth, width)
    pads = pad_rows.reshape(1, -1)
    win_weights = (win_query, win_key, win_value, win_out)
    grid_weights = (grid_query, grid_key, grid_value, grid_out)
    win_gain, grid_gain = win_gain.reshape(1, -1), grid_gain.reshape(1, -1)
    blocks, held = window_part(
        flat, pads, land_sea, win_gain, grid_gain, win_weights, grid_weights
    )
    mixed = exchange(grid_part(exchange(blocks), held))
    return final_part(mixed).reshape(height, breadth, width)


def solution(mesh):
    whole = P()
    split = P("lat", "lon", None)
    placed = (split, whole, split) + (whole,) * 10
    return jax.shard_map(local, mesh=mesh, in_specs=placed, out_specs=split, check_vma=False)
```

```python
import functools
import math

import jax
import jax.numpy as jnp
from jax import lax
from jax.experimental import pallas as pl
from jax.experimental.pallas import tpu as pltpu
from jax.sharding import PartitionSpec as P

HEADS = 16
GROUPS = 4
WIN = 8
SHIFT = 4
EPSILON = 1e-06
MASKED = -1e30
BF16 = jnp.bfloat16
F32 = jnp.float32
I32 = jnp.int32


def iota(shape, axis):
    return lax.broadcasted_iota(I32, shape, axis)


def one_hot(hits):
    return jnp.where(hits, 1.0, 0.0).astype(BF16)


def matmul(left, right):
    return jnp.dot(left, right, preferred_element_type=F32)


def matmul_nt(left, right):
    return lax.dot_general(left, right, (((1,), (1,)), ((), ())), preferred_element_type=F32)


def norm(rows, gain):
    mean_sq = jnp.mean(rows * rows, axis=-1, keepdims=True)
    return (rows * lax.rsqrt(mean_sq + EPSILON) * gain).astype(BF16)


def usable_bias(pad_ref, wanted_row):
    lanes = wanted_row.shape[1]
    pads = jnp.broadcast_to(pad_ref[...].astype(F32).astype(BF16), (16, pad_ref.shape[1]))
    picks = one_hot(iota((pad_ref.shape[1], lanes), 0) == wanted_row)
    return jnp.where(matmul(pads, picks)[:1] > 0.5, 0.0, MASKED)


def fetch(pairs, sems):
    copies = [
        pltpu.make_async_copy(source, target, sems.at[n]) for n, (source, target) in enumerate(pairs)
    ]
    for copy in copies:
        copy.start()
    return copies


def cross(upper, lower):
    first = iota((1, 8, 1), 1) < 4
    return (
        jnp.where(first, upper, jnp.roll(lower, 4, axis=1)),
        jnp.where(first, jnp.roll(upper, 4, axis=1), lower),
    )


def block_tiles(tiles):
    half = tiles.shape[2] // 2
    return jnp.stack(cross(tiles[:, :, :half], tiles[:, :, half:]), axis=1)


def project(rows, weight, target_ref, factor=None):
    product = matmul(rows, weight[...])
    if factor is not None:
        product = product * factor
    target_ref[...] = product.astype(BF16)


def query_factor(head_size):
    return math.log2(math.e) / math.sqrt(head_size)


def window_attention(bands, gate_of, pad_ref, q_ref, k_ref, v_ref, heads_ref):
    width = q_ref.shape[1]
    head_size = width // HEADS
    quad = 4 * head_size
    first = lax.axis_index("lat") * 16
    key_lane = iota((1, quad), 1) % 64
    biases = [usable_bias(pad_ref, first + band * 8 + key_lane // 8) for band in range(2)]
    head_lane = iota((1, quad), 1) // head_size
    masks = [one_hot(head_lane == h) for h in range(4)]
    ones = one_hot(iota((quad, quad), 0) // 64 == iota((quad, quad), 1) // head_size)
    lower = iota((1, 128), 1) < 64

    def spread(block):
        return jnp.concatenate([block * mask for mask in masks], axis=0)

    def weight_of(tile, group):
        span = slice(tile * 64, (tile + 1) * 64)
        lanes = slice(group * quad, (group + 1) * quad)
        scores = matmul_nt(q_ref[span, lanes], spread(k_ref[span, lanes])) + biases[bands[tile]]
        exps = []
        for block in range(2):
            part_scores = scores[:, block * 128 : (block + 1) * 128]
            low = jnp.max(jnp.where(lower, part_scores, -jnp.inf), axis=1, keepdims=True)
            high = jnp.max(jnp.where(lower, -jnp.inf, part_scores), axis=1, keepdims=True)
            exps.append(jnp.exp2(part_scores - jnp.where(lower, low, high)).astype(BF16))
        return jnp.concatenate(exps, axis=1)

    units = [(tile, group) for group in range(GROUPS) for tile in range(len(bands))]
    size = min(8, len(units))
    for start in range(0, len(units), size):
        batch = units[start : start + size]
        weights = [weight_of(*unit) for unit in batch]
        totals = matmul(jnp.concatenate(weights, axis=0), ones)
        for at, (tile, group) in enumerate(batch):
            span = slice(tile * 64, (tile + 1) * 64)
            lanes = slice(group * quad, (group + 1) * quad)
            total = totals[at * 64 : (at + 1) * 64]
            heads = matmul(weights[at], spread(v_ref[span, lanes])) / total * gate_of(tile, group)
            heads_ref[span, lanes] = heads.astype(BF16)


def swap_halves(tiles):
    return jnp.roll(tiles, 4, axis=1)


def project_kernel(
    tok_hbm, land_hbm, pad_hbm, gain_hbm, grid_gain_hbm, wq_hbm, wk_hbm, wv_hbm,
    halo_ref, x_ref, edge_ref, gate_ref, pad_ref, gain_ref, grid_gain_ref, wq_ref, wk_ref, wv_ref,
    normed_ref, q_ref,
    tok_ref, land_ref, sems,
):
    copies = fetch(
        [
            (tok_hbm, tok_ref), (land_hbm, land_ref), (gain_hbm, gain_ref),
            (pad_hbm, pad_ref), (grid_gain_hbm, grid_gain_ref),
            (wq_hbm, wq_ref), (wk_hbm, wk_ref), (wv_hbm, wv_ref),
        ],
        sems,
    )
    cells, width = tok_ref.shape
    rows = q_ref.shape[0]
    for copy in copies[:5]:
        copy.wait()
    tiles = tok_ref[...].astype(F32).reshape(16, 4, 8, width)
    first = iota((1, 8, 1), 1) < 4
    pairs = tiles[:, 3].reshape(8, 2, 8, width)
    halo = jnp.where(first, swap_halves(pairs[:, 0]), pairs[:, 1])
    halo_ref[0:64, :] = halo.reshape(64, width).astype(BF16)
    tile_at, group_at = iota((8, width), 0), iota((8, width), 1) // (width // GROUPS)
    gates = jnp.zeros((8, width), F32)
    for tile in range(8):
        for n in range(GROUPS):
            gate = land_ref[tile // 4, tile % 4, n].astype(F32)
            gates = jnp.where((tile_at == tile) & (group_at == n), gate, gates)
    gate_ref[...] = gates
    outer_gates = [gates[3:4], gates[7:8], jnp.zeros((14, width), F32)]
    halo_ref[64:80, :] = jnp.concatenate(outer_gates, axis=0).astype(BF16)
    edge_ref[...] = tiles[:, 0].reshape(128, width).astype(BF16)
    pieces = []
    for band in range(2):
        lines = slice(band * 8, band * 8 + 8)
        for tile_col in range(3):
            pieces.append(
                swap_halves(jnp.where(first, tiles[lines, tile_col + 1], tiles[lines, tile_col]))
            )
    x = jnp.concatenate(pieces, axis=0).reshape(rows, width)
    x_ref[...] = x
    normed = norm(x, gain_ref[...])
    normed_ref[...] = normed
    copies[5].wait()
    project(normed, wq_ref, q_ref, query_factor(width // HEADS))
    for copy in copies[6:]:
        copy.wait()


def inner_kernel(
    x_ref, normed_ref, q_ref, wk_ref, wv_ref, pad_ref, gate_ref,
    wo_hbm, gq_hbm, gk_hbm, gv_hbm, go_hbm,
    out_ref, wo_ref, gq_ref, gk_ref, gv_ref, go_ref,
    k_ref, v_ref, heads_ref, sems,
):
    copies = fetch(
        [
            (wo_hbm, wo_ref), (gq_hbm, gq_ref), (gk_hbm, gk_ref), (gv_hbm, gv_ref),
            (go_hbm, go_ref),
        ],
        sems,
    )
    rows, width = heads_ref.shape
    quad = width // GROUPS
    normed = normed_ref[...]
    project(normed, wk_ref, k_ref)
    project(normed, wv_ref, v_ref)

    def gate_of(tile, group):
        row = tile // 3 * 4 + tile % 3
        return gate_ref[row : row + 1, group * quad : (group + 1) * quad]

    window_attention([0, 0, 0, 1, 1, 1], gate_of, pad_ref, q_ref, k_ref, v_ref, heads_ref)
    copies[0].wait()
    after = x_ref[...] + matmul(heads_ref[...], wo_ref[...])
    blocks = block_tiles(after.reshape(rows // 8, 8, width))
    out_ref[...] = blocks.reshape(2 * rows, width // 2).astype(BF16)
    for copy in copies[1:]:
        copy.wait()


def outer_kernel(
    inner_ref, halo_ref, edge_ref, gain_ref, wq_ref, wk_ref, wv_ref, wo_ref, pad_ref,
    out_ref, q_ref, k_ref, v_ref, heads_ref,
):
    rows, width = heads_ref.shape
    first = iota((1, 8, 1), 1) < 4
    own = edge_ref[...].astype(F32).reshape(8, 2, 8, width)
    halo = halo_ref[0:64, :].astype(F32).reshape(8, 8, width)
    even = jnp.where(first, halo, swap_halves(own[:, 0]))
    odd = swap_halves(jnp.where(first, own[:, 1], halo))
    gates = halo_ref[64:80, :].astype(F32)
    x = jnp.stack([even, odd], axis=1).reshape(rows, width)
    normed = norm(x, gain_ref[...])
    project(normed, wq_ref, q_ref, query_factor(width // HEADS))
    project(normed, wk_ref, k_ref)
    project(normed, wv_ref, v_ref)

    def gate_of(tile, group):
        return gates[tile : tile + 1, group * (width // GROUPS) : (group + 1) * (width // GROUPS)]

    window_attention([0, 1], gate_of, pad_ref, q_ref, k_ref, v_ref, heads_ref)
    after = x + matmul(heads_ref[...], wo_ref[...])
    outer = block_tiles(after.reshape(16, 8, width))
    inner = inner_ref[...].astype(F32).reshape(2, 3, 8, 2, 8, width // 2)
    for band in range(2):
        lines = slice(band * 8, band * 8 + 8)
        ordered = [outer[lines, 1]]
        for tile_col in range(3):
            ordered += [inner[band, tile_col, :, 0], inner[band, tile_col, :, 1]]
        ordered.append(outer[lines, 0])
        blocks = jnp.stack(ordered, axis=1).reshape(512, width // 2)
        out_ref[band * 512 : (band + 1) * 512, :] = blocks.astype(BF16)


def in_hbm(arrays):
    return [pltpu.with_memory_space_constraint(a, pltpu.HBM) for a in arrays]


VMEM_SPEC = pl.BlockSpec(memory_space=pltpu.VMEM)
HBM_SPEC = pl.BlockSpec(memory_space=pltpu.HBM)


def call(kernel, name, outs, in_vmem, from_hbm, scratch, rows, exps):
    width = 1024
    return pl.pallas_call(
        kernel,
        out_shape=outs,
        in_specs=[VMEM_SPEC] * len(in_vmem) + [HBM_SPEC] * len(from_hbm),
        out_specs=[VMEM_SPEC] * len(outs),
        scratch_shapes=scratch,
        compiler_params=pltpu.CompilerParams(vmem_limit_bytes=28 * 2**20),
        cost_estimate=pl.CostEstimate(
            flops=8 * rows * width * width, bytes_accessed=10 * 2**20, transcendentals=exps
        ),
        name=name,
    )(*in_vmem, *in_hbm(from_hbm))


def window_part(tokens, pads, land_sea, gain, grid_gain, weights, grid_weights):
    cells, width = tokens.shape
    inner, outer = cells * 3 // 4, cells // 4
    weight = pltpu.VMEM((width, width), BF16)
    rows = pltpu.VMEM((inner, width), BF16)
    halo, x, edge, gates, pads_held, win_gain, gain_held, wq, wk, wv, normed, q = call(
        project_kernel,
        "window_project",
        [
            jax.ShapeDtypeStruct((cells // 8 + 16, width), BF16),
            pltpu.VMEM((inner, width), F32),
            pltpu.VMEM((outer, width), BF16),
            pltpu.VMEM((8, width), F32),
            pltpu.VMEM(pads.shape, I32),
            pltpu.VMEM(gain.shape, F32),
            pltpu.VMEM(grid_gain.shape, F32),
        ]
        + [weight] * 3
        + [rows] * 2,
        [],
        [tokens, land_sea, pads, gain, grid_gain, *weights[:3]],
        [
            pltpu.VMEM((cells, width), BF16),
            pltpu.SMEM(land_sea.shape, I32),
            pltpu.SemaphoreType.DMA((8,)),
        ],
        inner,
        0,
    )
    halo = from_behind(halo, "lon", 1)
    inside, wo, *grid_held = call(
        inner_kernel,
        "window_inner",
        [pltpu.VMEM((2 * inner, width // 2), BF16)] + [weight] * 5,
        [x, normed, q, wk, wv, pads_held, gates],
        [weights[3], *grid_weights],
        [rows] * 3 + [pltpu.SemaphoreType.DMA((5,))],
        inner,
        inner * 1024,
    )
    blocks = call(
        outer_kernel,
        "window_outer",
        [jax.ShapeDtypeStruct((2 * cells, width // 2), BF16)],
        [inside, halo, edge, win_gain, wq, wk, wv, wo, pads_held],
        [],
        [pltpu.VMEM((outer, width), BF16)] * 4,
        outer,
        outer * 1024,
    )[0]
    grid_held = [pads_held, gain_held, *grid_held]
    return blocks, grid_held


def grid_kernel(
    block_ref, pad_ref, gain_ref, wq_ref, wk_ref, wv_ref, wo_ref,
    out_ref, wide_ref, x_ref, normed_ref, q_ref, k_ref, v_ref, heads_ref,
):
    rows, width = q_ref.shape
    members = 128
    groups = rows // members
    head_size = width // HEADS
    pair = 2 * head_size
    chunks = wide_ref.shape[0]
    for chunk in range(chunks):
        wide_ref[chunk, : 2 * rows] = block_ref[:, chunk * 128 : (chunk + 1) * 128].astype(F32)
    lanes_of = [
        (slice(n * 128, (n + 1) * 128), n % chunks, n // chunks * groups)
        for n in range(2 * chunks)
    ]
    for group in range(groups):
        span = slice(group * members, (group + 1) * members)
        for lanes, chunk, start in lanes_of:
            x_ref[span, lanes] = wide_ref[chunk, pl.ds(start + group, members, stride=8), :]
        normed_ref[span, :] = norm(x_ref[span, :], gain_ref[...])
    normed = normed_ref[...]
    project(normed, wq_ref, q_ref, query_factor(head_size))
    project(normed, wk_ref, k_ref)
    project(normed, wv_ref, v_ref)
    key_lane = iota((1, 2 * members), 1) % members
    bias = usable_bias(pad_ref, (key_lane // 8) * 16 + lax.axis_index("lat"))
    masks = [one_hot(iota((1, pair), 1) // head_size == h) for h in range(2)]
    ones = one_hot(
        iota((2 * members, pair), 0) // members == iota((2 * members, pair), 1) // head_size
    )

    def spread(block):
        return jnp.concatenate([block * mask for mask in masks], axis=0)

    for group in range(groups):
        span = slice(group * members, (group + 1) * members)
        for two in range(HEADS // 2):
            lanes = slice(two * pair, (two + 1) * pair)
            scores = matmul_nt(q_ref[span, lanes], spread(k_ref[span, lanes])) + bias
            exps = []
            for half in range(2):
                head_scores = scores[:, half * members : (half + 1) * members]
                largest = jnp.max(head_scores, axis=1, keepdims=True)
                exps.append(jnp.exp2(head_scores - largest).astype(BF16))
            weight = jnp.concatenate(exps, axis=1)
            both = jnp.concatenate([spread(v_ref[span, lanes]), ones], axis=1)
            sums = matmul(weight, both)
            heads_ref[span, lanes] = (sums[:, :pair] / sums[:, pair:]).astype(BF16)
    wrapped = lax.axis_index("lon") == lax.axis_size("lon") - 1
    mixed = x_ref[...] + matmul(heads_ref[...], wo_ref[...])
    for group in range(groups):
        span = slice(group * members, (group + 1) * members)
        tiles = mixed[span].reshape(members // 8, 8, width)
        home = jnp.where(wrapped, jnp.roll(tiles, -1, axis=1), tiles).reshape(members, width)
        for lanes, chunk, start in lanes_of:
            wide_ref[chunk, pl.ds(start + group, members, stride=8), :] = home[:, lanes]
    for chunk in range(chunks):
        out_ref[:, chunk * 128 : (chunk + 1) * 128] = wide_ref[chunk, : 2 * rows].astype(BF16)


def grid_part(blocks, held):
    rows, width = blocks.shape[0] // 2, blocks.shape[1] * 2
    return call(
        grid_kernel,
        "grid_part",
        [jax.ShapeDtypeStruct(blocks.shape, BF16)],
        [blocks, *held],
        [],
        [
            pltpu.VMEM((blocks.shape[1] // 128, blocks.shape[0] + 8, 128), F32),
            pltpu.VMEM((rows, width), F32),
        ]
        + [pltpu.VMEM((rows, width), BF16)] * 5,
        rows,
        rows * 2048,
    )[0]


def final_kernel(block_ref, out_hbm, out_ref, sems):
    rows, width = out_ref.shape
    steps = 4
    part = rows // steps
    copies = []
    for step in range(steps):
        span = slice(step * part, (step + 1) * part)
        blocks = block_ref[2 * step * part : 2 * (step + 1) * part, :].astype(F32)
        tiles = blocks.reshape(part // 8, 2, 8, width // 2)
        whole = jnp.concatenate(cross(tiles[:, 0], tiles[:, 1]), axis=2)
        out_ref[span, :] = whole.reshape(part, width).astype(BF16)
        copy = pltpu.make_async_copy(out_ref.at[span], out_hbm.at[span], sems.at[step])
        copy.start()
        copies.append(copy)
    for copy in copies:
        copy.wait()


def final_part(blocks):
    rows, width = blocks.shape[0] // 2, blocks.shape[1] * 2
    return pl.pallas_call(
        final_kernel,
        out_shape=jax.ShapeDtypeStruct((rows, width), BF16),
        in_specs=[VMEM_SPEC],
        out_specs=HBM_SPEC,
        scratch_shapes=[pltpu.VMEM((rows, width), BF16), pltpu.SemaphoreType.DMA((4,))],
        compiler_params=pltpu.CompilerParams(vmem_limit_bytes=16 * 2**20),
        name="final_part",
    )(blocks)


def from_behind(block, axis, distance):
    devices = range(lax.axis_size(axis))
    route = [((i - distance) % len(devices), i) for i in devices]
    return lax.ppermute(block, axis, route)


def exchange(blocks):
    count, width = blocks.shape
    members = lax.axis_size("lat") * lax.axis_size("lon")
    split = blocks.reshape(members, count // members, width)
    moved = lax.all_to_all(split, ("lat", "lon"), split_axis=0, concat_axis=0, tiled=True)
    return moved.reshape(count, width)


def local(
    tokens,
    pad_rows,
    land_sea,
    win_gain,
    win_query,
    win_key,
    win_value,
    win_out,
    grid_gain,
    grid_query,
    grid_key,
    grid_value,
    grid_out,
):
    height, breadth, width = tokens.shape
    flat = tokens.reshape(height * breadth, width)
    pads = pad_rows.reshape(1, -1)
    win_weights = (win_query, win_key, win_value, win_out)
    grid_weights = (grid_query, grid_key, grid_value, grid_out)
    win_gain, grid_gain = win_gain.reshape(1, -1), grid_gain.reshape(1, -1)
    blocks, held = window_part(
        flat, pads, land_sea, win_gain, grid_gain, win_weights, grid_weights
    )
    mixed = exchange(grid_part(exchange(blocks), held))
    return final_part(mixed).reshape(height, breadth, width)


def solution(mesh):
    whole = P()
    split = P("lat", "lon", None)
    placed = (split, whole, split) + (whole,) * 10
    return jax.shard_map(local, mesh=mesh, in_specs=placed, out_specs=split, check_vma=False)
```

```python
import functools
import math

import jax
import jax.numpy as jnp
from jax import lax
from jax.experimental import pallas as pl
from jax.experimental.pallas import tpu as pltpu
from jax.sharding import PartitionSpec as P

HEADS = 16
GROUPS = 4
WIN = 8
SHIFT = 4
EPSILON = 1e-06
MASKED = -1e30
BF16 = jnp.bfloat16
F32 = jnp.float32
I32 = jnp.int32


def iota(shape, axis):
    return lax.broadcasted_iota(I32, shape, axis)


def one_hot(hits):
    return jnp.where(hits, 1.0, 0.0).astype(BF16)


def matmul(left, right):
    return jnp.dot(left, right, preferred_element_type=F32)


def matmul_nt(left, right):
    return lax.dot_general(left, right, (((1,), (1,)), ((), ())), preferred_element_type=F32)


def norm(rows, gain):
    mean_sq = jnp.mean(rows * rows, axis=-1, keepdims=True)
    return (rows * lax.rsqrt(mean_sq + EPSILON) * gain).astype(BF16)


def usable_bias(pad_ref, wanted_row):
    lanes = wanted_row.shape[1]
    pads = jnp.broadcast_to(pad_ref[...].astype(F32).astype(BF16), (16, pad_ref.shape[1]))
    picks = one_hot(iota((pad_ref.shape[1], lanes), 0) == wanted_row)
    return jnp.where(matmul(pads, picks)[:1] > 0.5, 0.0, MASKED)


def fetch(pairs, sems):
    copies = [
        pltpu.make_async_copy(source, target, sems.at[n]) for n, (source, target) in enumerate(pairs)
    ]
    for copy in copies:
        copy.start()
    return copies


def cross(upper, lower):
    first = iota((1, 8, 1), 1) < 4
    return (
        jnp.where(first, upper, jnp.roll(lower, 4, axis=1)),
        jnp.where(first, jnp.roll(upper, 4, axis=1), lower),
    )


def block_tiles(tiles):
    half = tiles.shape[2] // 2
    return jnp.stack(cross(tiles[:, :, :half], tiles[:, :, half:]), axis=1)


def project(rows, weight, target_ref, factor=None):
    product = matmul(rows, weight[...])
    if factor is not None:
        product = product * factor
    target_ref[...] = product.astype(BF16)


def query_factor(head_size):
    return math.log2(math.e) / math.sqrt(head_size)


def window_attention(bands, gate_of, pad_ref, q_ref, k_ref, v_ref, heads_ref):
    width = q_ref.shape[1]
    head_size = width // HEADS
    quad = 4 * head_size
    first = lax.axis_index("lat") * 16
    key_lane = iota((1, quad), 1) % 64
    biases = [usable_bias(pad_ref, first + band * 8 + key_lane // 8) for band in range(2)]
    head_lane = iota((1, quad), 1) // head_size
    masks = [one_hot(head_lane == h) for h in range(4)]
    ones = one_hot(iota((quad, quad), 0) // 64 == iota((quad, quad), 1) // head_size)
    lower = iota((1, 128), 1) < 64

    def spread(block):
        return jnp.concatenate([block * mask for mask in masks], axis=0)

    def weight_of(tile, group):
        span = slice(tile * 64, (tile + 1) * 64)
        lanes = slice(group * quad, (group + 1) * quad)
        scores = matmul_nt(q_ref[span, lanes], spread(k_ref[span, lanes])) + biases[bands[tile]]
        exps = []
        for block in range(2):
            part_scores = scores[:, block * 128 : (block + 1) * 128]
            low = jnp.max(jnp.where(lower, part_scores, -jnp.inf), axis=1, keepdims=True)
            high = jnp.max(jnp.where(lower, -jnp.inf, part_scores), axis=1, keepdims=True)
            exps.append(jnp.exp2(part_scores - jnp.where(lower, low, high)).astype(BF16))
        return jnp.concatenate(exps, axis=1)

    units = [(tile, group) for group in range(GROUPS) for tile in range(len(bands))]
    size = min(8, len(units))
    batches = [units[at : at + size] for at in range(0, len(units), size)]

    def finish(batch, weights):
        totals = matmul(jnp.concatenate(weights, axis=0), ones)
        for at, (tile, group) in enumerate(batch):
            span = slice(tile * 64, (tile + 1) * 64)
            lanes = slice(group * quad, (group + 1) * quad)
            total = totals[at * 64 : (at + 1) * 64]
            heads = matmul(weights[at], spread(v_ref[span, lanes])) / total * gate_of(tile, group)
            heads_ref[span, lanes] = heads.astype(BF16)

    last = None
    for batch in batches:
        weights = [weight_of(*unit) for unit in batch]
        if last is not None:
            finish(*last)
        last = (batch, weights)
    finish(*last)


def swap_halves(tiles):
    return jnp.roll(tiles, 4, axis=1)


def project_kernel(
    tok_hbm, land_hbm, pad_hbm, gain_hbm, grid_gain_hbm, wq_hbm, wk_hbm, wv_hbm,
    halo_ref, x_ref, edge_ref, gate_ref, pad_ref, gain_ref, grid_gain_ref, wq_ref, wk_ref, wv_ref,
    normed_ref, q_ref,
    tok_ref, land_ref, sems,
):
    copies = fetch(
        [
            (tok_hbm, tok_ref), (land_hbm, land_ref), (gain_hbm, gain_ref),
            (pad_hbm, pad_ref), (grid_gain_hbm, grid_gain_ref),
            (wq_hbm, wq_ref), (wk_hbm, wk_ref), (wv_hbm, wv_ref),
        ],
        sems,
    )
    cells, width = tok_ref.shape
    rows = q_ref.shape[0]
    for copy in copies[:5]:
        copy.wait()
    tiles = tok_ref[...].astype(F32).reshape(16, 4, 8, width)
    first = iota((1, 8, 1), 1) < 4
    pairs = tiles[:, 3].reshape(8, 2, 8, width)
    halo = jnp.where(first, swap_halves(pairs[:, 0]), pairs[:, 1])
    halo_ref[0:64, :] = halo.reshape(64, width).astype(BF16)
    tile_at, group_at = iota((8, width), 0), iota((8, width), 1) // (width // GROUPS)
    gates = jnp.zeros((8, width), F32)
    for tile in range(8):
        for n in range(GROUPS):
            gate = land_ref[tile // 4, tile % 4, n].astype(F32)
            gates = jnp.where((tile_at == tile) & (group_at == n), gate, gates)
    gate_ref[...] = gates
    outer_gates = [gates[3:4], gates[7:8], jnp.zeros((14, width), F32)]
    halo_ref[64:80, :] = jnp.concatenate(outer_gates, axis=0).astype(BF16)
    edge_ref[...] = tiles[:, 0].reshape(128, width).astype(BF16)
    pieces = []
    for band in range(2):
        lines = slice(band * 8, band * 8 + 8)
        for tile_col in range(3):
            pieces.append(
                swap_halves(jnp.where(first, tiles[lines, tile_col + 1], tiles[lines, tile_col]))
            )
    x = jnp.concatenate(pieces, axis=0).reshape(rows, width)
    x_ref[...] = x
    normed = norm(x, gain_ref[...])
    normed_ref[...] = normed
    copies[5].wait()
    project(normed, wq_ref, q_ref, query_factor(width // HEADS))
    for copy in copies[6:]:
        copy.wait()


def inner_kernel(
    x_ref, normed_ref, q_ref, wk_ref, wv_ref, pad_ref, gate_ref,
    wo_hbm, gq_hbm, gk_hbm, gv_hbm, go_hbm,
    out_ref, wo_ref, gq_ref, gk_ref, gv_ref, go_ref,
    k_ref, v_ref, heads_ref, sems,
):
    copies = fetch(
        [
            (wo_hbm, wo_ref), (gq_hbm, gq_ref), (gk_hbm, gk_ref), (gv_hbm, gv_ref),
            (go_hbm, go_ref),
        ],
        sems,
    )
    rows, width = heads_ref.shape
    quad = width // GROUPS
    normed = normed_ref[...]
    project(normed, wk_ref, k_ref)
    project(normed, wv_ref, v_ref)

    def gate_of(tile, group):
        row = tile // 3 * 4 + tile % 3
        return gate_ref[row : row + 1, group * quad : (group + 1) * quad]

    window_attention([0, 0, 0, 1, 1, 1], gate_of, pad_ref, q_ref, k_ref, v_ref, heads_ref)
    copies[0].wait()
    after = x_ref[...] + matmul(heads_ref[...], wo_ref[...])
    blocks = block_tiles(after.reshape(rows // 8, 8, width))
    out_ref[...] = blocks.reshape(2 * rows, width // 2).astype(BF16)
    for copy in copies[1:]:
        copy.wait()


def outer_kernel(
    inner_ref, halo_ref, edge_ref, gain_ref, wq_ref, wk_ref, wv_ref, wo_ref, pad_ref,
    out_ref, q_ref, k_ref, v_ref, heads_ref,
):
    rows, width = heads_ref.shape
    first = iota((1, 8, 1), 1) < 4
    own = edge_ref[...].astype(F32).reshape(8, 2, 8, width)
    halo = halo_ref[0:64, :].astype(F32).reshape(8, 8, width)
    even = jnp.where(first, halo, swap_halves(own[:, 0]))
    odd = swap_halves(jnp.where(first, own[:, 1], halo))
    gates = halo_ref[64:80, :].astype(F32)
    x = jnp.stack([even, odd], axis=1).reshape(rows, width)
    normed = norm(x, gain_ref[...])
    project(normed, wq_ref, q_ref, query_factor(width // HEADS))
    project(normed, wk_ref, k_ref)
    project(normed, wv_ref, v_ref)

    def gate_of(tile, group):
        return gates[tile : tile + 1, group * (width // GROUPS) : (group + 1) * (width // GROUPS)]

    window_attention([0, 1], gate_of, pad_ref, q_ref, k_ref, v_ref, heads_ref)
    after = x + matmul(heads_ref[...], wo_ref[...])
    outer = block_tiles(after.reshape(16, 8, width))
    inner = inner_ref[...].astype(F32).reshape(2, 3, 8, 2, 8, width // 2)
    for band in range(2):
        lines = slice(band * 8, band * 8 + 8)
        ordered = [outer[lines, 1]]
        for tile_col in range(3):
            ordered += [inner[band, tile_col, :, 0], inner[band, tile_col, :, 1]]
        ordered.append(outer[lines, 0])
        blocks = jnp.stack(ordered, axis=1).reshape(512, width // 2)
        out_ref[band * 512 : (band + 1) * 512, :] = blocks.astype(BF16)


def in_hbm(arrays):
    return [pltpu.with_memory_space_constraint(a, pltpu.HBM) for a in arrays]


VMEM_SPEC = pl.BlockSpec(memory_space=pltpu.VMEM)
HBM_SPEC = pl.BlockSpec(memory_space=pltpu.HBM)


def call(kernel, name, outs, in_vmem, from_hbm, scratch, rows, exps):
    width = 1024
    return pl.pallas_call(
        kernel,
        out_shape=outs,
        in_specs=[VMEM_SPEC] * len(in_vmem) + [HBM_SPEC] * len(from_hbm),
        out_specs=[VMEM_SPEC] * len(outs),
        scratch_shapes=scratch,
        compiler_params=pltpu.CompilerParams(vmem_limit_bytes=28 * 2**20),
        cost_estimate=pl.CostEstimate(
            flops=8 * rows * width * width, bytes_accessed=10 * 2**20, transcendentals=exps
        ),
        name=name,
    )(*in_vmem, *in_hbm(from_hbm))


def window_part(tokens, pads, land_sea, gain, grid_gain, weights, grid_weights):
    cells, width = tokens.shape
    inner, outer = cells * 3 // 4, cells // 4
    weight = pltpu.VMEM((width, width), BF16)
    rows = pltpu.VMEM((inner, width), BF16)
    halo, x, edge, gates, pads_held, win_gain, gain_held, wq, wk, wv, normed, q = call(
        project_kernel,
        "window_project",
        [
            jax.ShapeDtypeStruct((cells // 8 + 16, width), BF16),
            pltpu.VMEM((inner, width), F32),
            pltpu.VMEM((outer, width), BF16),
            pltpu.VMEM((8, width), F32),
            pltpu.VMEM(pads.shape, I32),
            pltpu.VMEM(gain.shape, F32),
            pltpu.VMEM(grid_gain.shape, F32),
        ]
        + [weight] * 3
        + [rows] * 2,
        [],
        [tokens, land_sea, pads, gain, grid_gain, *weights[:3]],
        [
            pltpu.VMEM((cells, width), BF16),
            pltpu.SMEM(land_sea.shape, I32),
            pltpu.SemaphoreType.DMA((8,)),
        ],
        inner,
        0,
    )
    halo = from_behind(halo, "lon", 1)
    inside, wo, *grid_held = call(
        inner_kernel,
        "window_inner",
        [pltpu.VMEM((2 * inner, width // 2), BF16)] + [weight] * 5,
        [x, normed, q, wk, wv, pads_held, gates],
        [weights[3], *grid_weights],
        [rows] * 3 + [pltpu.SemaphoreType.DMA((5,))],
        inner,
        inner * 1024,
    )
    blocks = call(
        outer_kernel,
        "window_outer",
        [jax.ShapeDtypeStruct((2 * cells, width // 2), BF16)],
        [inside, halo, edge, win_gain, wq, wk, wv, wo, pads_held],
        [],
        [pltpu.VMEM((outer, width), BF16)] * 4,
        outer,
        outer * 1024,
    )[0]
    grid_held = [pads_held, gain_held, *grid_held]
    return blocks, grid_held


def grid_kernel(
    block_ref, pad_ref, gain_ref, wq_ref, wk_ref, wv_ref, wo_ref,
    out_ref, wide_ref, x_ref, normed_ref, q_ref, k_ref, v_ref, heads_ref,
):
    rows, width = q_ref.shape
    members = 128
    groups = rows // members
    head_size = width // HEADS
    pair = 2 * head_size
    chunks = wide_ref.shape[0]
    for chunk in range(chunks):
        wide_ref[chunk, : 2 * rows] = block_ref[:, chunk * 128 : (chunk + 1) * 128].astype(F32)
    lanes_of = [
        (slice(n * 128, (n + 1) * 128), n % chunks, n // chunks * groups)
        for n in range(2 * chunks)
    ]
    for group in range(groups):
        span = slice(group * members, (group + 1) * members)
        for lanes, chunk, start in lanes_of:
            x_ref[span, lanes] = wide_ref[chunk, pl.ds(start + group, members, stride=8), :]
        normed_ref[span, :] = norm(x_ref[span, :], gain_ref[...])
    normed = normed_ref[...]
    project(normed, wq_ref, q_ref, query_factor(head_size))
    project(normed, wk_ref, k_ref)
    project(normed, wv_ref, v_ref)
    key_lane = iota((1, 2 * members), 1) % members
    bias = usable_bias(pad_ref, (key_lane // 8) * 16 + lax.axis_index("lat"))
    masks = [one_hot(iota((1, pair), 1) // head_size == h) for h in range(2)]
    ones = one_hot(
        iota((2 * members, pair), 0) // members == iota((2 * members, pair), 1) // head_size
    )

    def spread(block):
        return jnp.concatenate([block * mask for mask in masks], axis=0)

    for group in range(groups):
        span = slice(group * members, (group + 1) * members)
        for two in range(HEADS // 2):
            lanes = slice(two * pair, (two + 1) * pair)
            scores = matmul_nt(q_ref[span, lanes], spread(k_ref[span, lanes])) + bias
            exps = []
            for half in range(2):
                head_scores = scores[:, half * members : (half + 1) * members]
                largest = jnp.max(head_scores, axis=1, keepdims=True)
                exps.append(jnp.exp2(head_scores - largest).astype(BF16))
            weight = jnp.concatenate(exps, axis=1)
            both = jnp.concatenate([spread(v_ref[span, lanes]), ones], axis=1)
            sums = matmul(weight, both)
            heads_ref[span, lanes] = (sums[:, :pair] / sums[:, pair:]).astype(BF16)
    wrapped = lax.axis_index("lon") == lax.axis_size("lon") - 1
    mixed = x_ref[...] + matmul(heads_ref[...], wo_ref[...])
    for group in range(groups):
        span = slice(group * members, (group + 1) * members)
        tiles = mixed[span].reshape(members // 8, 8, width)
        home = jnp.where(wrapped, jnp.roll(tiles, -1, axis=1), tiles).reshape(members, width)
        for lanes, chunk, start in lanes_of:
            wide_ref[chunk, pl.ds(start + group, members, stride=8), :] = home[:, lanes]
    for chunk in range(chunks):
        out_ref[:, chunk * 128 : (chunk + 1) * 128] = wide_ref[chunk, : 2 * rows].astype(BF16)


def grid_part(blocks, held):
    rows, width = blocks.shape[0] // 2, blocks.shape[1] * 2
    return call(
        grid_kernel,
        "grid_part",
        [jax.ShapeDtypeStruct(blocks.shape, BF16)],
        [blocks, *held],
        [],
        [
            pltpu.VMEM((blocks.shape[1] // 128, blocks.shape[0] + 8, 128), F32),
            pltpu.VMEM((rows, width), F32),
        ]
        + [pltpu.VMEM((rows, width), BF16)] * 5,
        rows,
        rows * 2048,
    )[0]


def final_kernel(block_ref, out_hbm, out_ref, sems):
    rows, width = out_ref.shape
    steps = 4
    part = rows // steps
    copies = []
    for step in range(steps):
        span = slice(step * part, (step + 1) * part)
        blocks = block_ref[2 * step * part : 2 * (step + 1) * part, :].astype(F32)
        tiles = blocks.reshape(part // 8, 2, 8, width // 2)
        whole = jnp.concatenate(cross(tiles[:, 0], tiles[:, 1]), axis=2)
        out_ref[span, :] = whole.reshape(part, width).astype(BF16)
        copy = pltpu.make_async_copy(out_ref.at[span], out_hbm.at[span], sems.at[step])
        copy.start()
        copies.append(copy)
    for copy in copies:
        copy.wait()


def final_part(blocks):
    rows, width = blocks.shape[0] // 2, blocks.shape[1] * 2
    return pl.pallas_call(
        final_kernel,
        out_shape=jax.ShapeDtypeStruct((rows, width), BF16),
        in_specs=[VMEM_SPEC],
        out_specs=HBM_SPEC,
        scratch_shapes=[pltpu.VMEM((rows, width), BF16), pltpu.SemaphoreType.DMA((4,))],
        compiler_params=pltpu.CompilerParams(vmem_limit_bytes=16 * 2**20),
        name="final_part",
    )(blocks)


def from_behind(block, axis, distance):
    devices = range(lax.axis_size(axis))
    route = [((i - distance) % len(devices), i) for i in devices]
    return lax.ppermute(block, axis, route)


def exchange(blocks):
    count, width = blocks.shape
    members = lax.axis_size("lat") * lax.axis_size("lon")
    split = blocks.reshape(members, count // members, width)
    moved = lax.all_to_all(split, ("lat", "lon"), split_axis=0, concat_axis=0, tiled=True)
    return moved.reshape(count, width)


def local(
    tokens,
    pad_rows,
    land_sea,
    win_gain,
    win_query,
    win_key,
    win_value,
    win_out,
    grid_gain,
    grid_query,
    grid_key,
    grid_value,
    grid_out,
):
    height, breadth, width = tokens.shape
    flat = tokens.reshape(height * breadth, width)
    pads = pad_rows.reshape(1, -1)
    win_weights = (win_query, win_key, win_value, win_out)
    grid_weights = (grid_query, grid_key, grid_value, grid_out)
    win_gain, grid_gain = win_gain.reshape(1, -1), grid_gain.reshape(1, -1)
    blocks, held = window_part(
        flat, pads, land_sea, win_gain, grid_gain, win_weights, grid_weights
    )
    mixed = exchange(grid_part(exchange(blocks), held))
    return final_part(mixed).reshape(height, breadth, width)


def solution(mesh):
    whole = P()
    split = P("lat", "lon", None)
    placed = (split, whole, split) + (whole,) * 10
    return jax.shard_map(local, mesh=mesh, in_specs=placed, out_specs=split, check_vma=False)
```
